512 devices in a mesh: dp: 128 (over y, z, core), sp: 4 (over x).
Axes of the slice: x: 4, y: 4, z: 16, core: 2. Of those that a mesh axis runs over, the one named last changes fastest.
Arguments:
- queries: bfloat16 [65536, 3584], P(('dp', 'sp')), may hold values from -128 to 128
- keys: bfloat16 [65536, 512], P(('dp', 'sp')), may hold values from -6 to 6
- values: bfloat16 [65536, 512], P(('dp', 'sp')), may hold values from -6 to 6
- document_lengths: int32 [128, 8], P('dp'), may hold values from 1 to 256, 512 in all within a row
- pair_ids: int32 [1024], P('dp'), may hold values from 0 to 1023, as said below
Outputs:
- embeddings: bfloat16 [1024, 3584], P('dp', 'sp')
- grads: float32 [1024, 3584], P('dp', 'sp')
The draws below stay inside these ranges and needn't reach their ends.
Inputs may be any that keep to these rules, and one draw needn't show every extreme that they name: `document_lengths`: each row's 8 lengths sum to 512; the longest is exactly 256. pair_ids pairs the 1024 documents two by two: pair_ids[pair_ids[i]] = i and pair_ids[i] != i.
All inputs are finite; a program needn't handle non-finite values.
Results may differ from the reference program's by a relative error of at most 0.0055.
Values may be sent and summed in bfloat16 or wider, within the bound.
A program may use at most 64 MiB of HBM per device.

```python
import math
import jax
import jax.numpy as jnp
import numpy as np
from jax import lax

QUERY_HEADS = 28
KEY_VALUE_HEADS = 4
HEAD_SIZE = 128
DOCS = 8
WINDOW_TOKENS = 512
LONGEST = 256
NDOC = 1024
BATCH_TOKENS = 65536
N_DP = 128


def key_field(key):
    return jnp.clip(jax.random.normal(key, (BATCH_TOKENS, KEY_VALUE_HEADS, HEAD_SIZE), jnp.float32), -6.0, 6.0)


def draw_keys(key, part):
    base_offset = key_field(key)
    return base_offset.reshape(BATCH_TOKENS, KEY_VALUE_HEADS * HEAD_SIZE).astype(jnp.bfloat16)


def draw_queries(key, part):
    key = jax.random.fold_in(key, 5)
    first_token = jax.random.fold_in(key, 0)
    random_noise = jnp.clip(jax.random.normal(first_token, (BATCH_TOKENS, KEY_VALUE_HEADS, QUERY_HEADS // KEY_VALUE_HEADS, HEAD_SIZE), jnp.float32), -6.0, 6.0)
    return random_noise.reshape(BATCH_TOKENS, QUERY_HEADS * HEAD_SIZE).astype(jnp.bfloat16)


def draw_pair_ids(key, part):
    key = jax.random.fold_in(key, 7)
    order = jax.random.permutation(key, NDOC).astype(jnp.int32)
    halves = order.reshape(NDOC // 2, 2)
    partner = jnp.zeros((NDOC,), jnp.int32)
    partner = partner.at[halves[:, 0]].set(halves[:, 1])
    partner = partner.at[halves[:, 1]].set(halves[:, 0])
    return partner


def block_scale(rng, dims, pieces, smallest, top_value):
    def one(position, parts):
        heights = jax.random.uniform(jax.random.fold_in(jax.random.fold_in(rng, 6), position), (parts,), jnp.float32, smallest / len(pieces), top_value / len(pieces))
        return jnp.repeat(jnp.exp(heights), dims[position] // parts).reshape((-1,) + (1,) * (len(dims) - position - 1))

    factor_of = one(*pieces[0])
    for cut in pieces[1:]:
        factor_of = factor_of * one(*cut)
    return factor_of


def split_up(number_of, total, most, skew):
    weights = [(1 << 20) // math.isqrt(grade ** skew) + 1 for grade in range(2, number_of + 1)]
    rest, counts = total - most - (number_of - 1), [1] * (number_of - 1)
    while rest > 0:
        movable = [i for i in range(number_of - 1) if counts[i] < most]
        whole, left = sum([weights[i] for i in movable]), rest
        for i in movable:
            more = min(most - counts[i], max(1, left * weights[i] // whole), rest)
            counts[i] = counts[i] + more
            rest = rest - more
    return np.array([most] + counts)


def uneven(stream_key, amount, total, reach, skew):
    if amount == 2:
        one = jax.random.randint(stream_key, (), max(1, total - reach), min(reach, total - 1) + 1)
        return jnp.stack([one, total - one])
    sizes = jnp.asarray(split_up(amount, total, reach, skew), jnp.int32)
    couples = (amount - 1) // 2
    source_of, sink = sizes[1:1 + 2 * couples:2], sizes[2:2 + 2 * couples:2]
    margin = jnp.minimum(source_of - 1, reach - sink)
    shifted = jax.random.randint(jax.random.fold_in(stream_key, 1), (couples,), 0, 1 << 20) % (margin + 1)
    sizes = sizes.at[1:1 + 2 * couples:2].set(source_of - shifted).at[2:2 + 2 * couples:2].set(sink + shifted)
    return sizes[jax.random.permutation(jax.random.fold_in(stream_key, 2), amount)]


def scatter_about(stream_key, dims, spread, reach, cuts=(), kind=jnp.bfloat16):
    loudness = block_scale(stream_key, dims, cuts, -0.22, 0.18) if cuts else 1.0
    values = jax.random.normal(stream_key, dims, jnp.float32) * spread * loudness
    return jnp.minimum(jnp.maximum(values, -reach), reach).astype(kind)


def setup_inputs(seed: int = 0) -> dict:
    arg_keys = jax.random.split(jax.random.key(seed), 6)
    queries = draw_queries(jax.random.fold_in(arg_keys[5], 71), 0)
    keys = draw_keys(jax.random.fold_in(arg_keys[5], 71), 0)
    values = scatter_about(arg_keys[2], (BATCH_TOKENS, KEY_VALUE_HEADS * HEAD_SIZE), 1.0, 6.0, ((0, 512),))
    document_lengths = jax.vmap(lambda own: uneven(own, DOCS, WINDOW_TOKENS, LONGEST, 2))(jax.random.split(arg_keys[3], N_DP)).reshape((N_DP, DOCS)).astype(jnp.int32)
    pair_ids = draw_pair_ids(jax.random.fold_in(arg_keys[5], 71), 0)
    return {"queries": queries, "keys": keys, "values": values, "document_lengths": document_lengths, "pair_ids": pair_ids}


SOFTMAX_TEMP = 0.02

def segment_of(lengths, count):
    ends = jnp.cumsum(lengths).astype(jnp.int32)
    places = jnp.arange(count, dtype=jnp.int32)
    return lax.optimization_barrier(jnp.sum((places[:, None] >= ends[None, :]).astype(jnp.int32), axis=1)).astype(jnp.int32)

def attend_head(query_flat, row_segment, key_head, value_head, segment):
    scores = jnp.dot(query_flat, key_head.T, preferred_element_type=jnp.float32) * HEAD_SIZE ** (-0.5)
    scores = jnp.where(row_segment[:, None] == segment[None, :], scores, -jnp.inf)
    largest = lax.optimization_barrier(jnp.max(scores, axis=1, keepdims=True))
    weights = jnp.exp(scores - largest)
    probs = (weights / lax.optimization_barrier(jnp.sum(weights, axis=1, keepdims=True))).astype(jnp.bfloat16)
    return jnp.dot(probs, value_head, preferred_element_type=jnp.float32).astype(jnp.bfloat16)

def pool_row(inputs):
    query_window_row, key_window_row, value_window_row, lengths = inputs
    head_group = QUERY_HEADS // KEY_VALUE_HEADS
    segment = segment_of(lengths, WINDOW_TOKENS)
    row_segment = jnp.repeat(segment, head_group)
    query_head_rows = query_window_row.reshape(WINDOW_TOKENS, KEY_VALUE_HEADS, head_group, HEAD_SIZE)
    key_head_rows = key_window_row.reshape(WINDOW_TOKENS, KEY_VALUE_HEADS, HEAD_SIZE)
    value_head_rows = value_window_row.reshape(WINDOW_TOKENS, KEY_VALUE_HEADS, HEAD_SIZE)
    outputs = []
    for head_number in range(KEY_VALUE_HEADS):
        flat = query_head_rows[:, head_number].reshape(WINDOW_TOKENS * head_group, HEAD_SIZE)
        result = attend_head(flat, row_segment, key_head_rows[:, head_number], value_head_rows[:, head_number], segment)
        outputs.append(result.reshape(WINDOW_TOKENS, head_group, HEAD_SIZE))
    attended = jnp.stack(outputs, axis=1).reshape(WINDOW_TOKENS, QUERY_HEADS * HEAD_SIZE)
    onehot = (segment[None, :] == jnp.arange(DOCS, dtype=jnp.int32)[:, None]).astype(jnp.bfloat16)
    summed = jnp.dot(onehot, attended, preferred_element_type=jnp.float32)
    return summed / lengths[:, None].astype(jnp.float32)

def reference(queries, keys, values, document_lengths, pair_ids):
    packed_rows = (queries.reshape(N_DP, WINDOW_TOKENS, QUERY_HEADS * HEAD_SIZE), keys.reshape(N_DP, WINDOW_TOKENS, KEY_VALUE_HEADS * HEAD_SIZE), values.reshape(N_DP, WINDOW_TOKENS, KEY_VALUE_HEADS * HEAD_SIZE), document_lengths)
    pooled = lax.map(pool_row, packed_rows).reshape(NDOC, QUERY_HEADS * HEAD_SIZE)
    radius = jnp.sqrt(lax.optimization_barrier(jnp.sum(pooled * pooled, axis=1, keepdims=True)) + 1e-06)
    embeddings = (pooled / radius).astype(jnp.bfloat16)
    wide_layout = embeddings.astype(jnp.float32)
    score_logits = jnp.dot(embeddings, embeddings.T, preferred_element_type=jnp.float32) / SOFTMAX_TEMP
    places = jnp.arange(NDOC, dtype=jnp.int32)
    score_logits = jnp.where(places[:, None] == places[None, :], -jnp.inf, score_logits)
    largest = lax.optimization_barrier(jnp.max(score_logits, axis=1, keepdims=True))
    weights = jnp.exp(score_logits - largest)
    probs = weights / lax.optimization_barrier(jnp.sum(weights, axis=1, keepdims=True))
    loss_coefficient = probs - (places[None, :] == pair_ids[:, None]).astype(jnp.float32)
    embedding_gradient = (jnp.dot(loss_coefficient, wide_layout, precision=lax.Precision.HIGHEST) + jnp.dot(loss_coefficient.T, wide_layout, precision=lax.Precision.HIGHEST)) / SOFTMAX_TEMP
    along = lax.optimization_barrier(jnp.sum(wide_layout * embedding_gradient, axis=1, keepdims=True))
    grads = (embedding_gradient - wide_layout * along) / radius
    return (embeddings, grads)
```

```python
import functools
import math

import jax
import jax.numpy as jnp
from jax import lax
from jax.experimental import pallas as pl
from jax.experimental.pallas import tpu as pltpu
from jax.sharding import PartitionSpec as P

MESH = pl.DeviceIdType.MESH
F32 = jnp.float32
BF16 = jnp.bfloat16
NT = (((1,), (1,)), ((), ()))

GROUPS = 4
PER = 7
HEADS = GROUPS * PER
D = 128
DOCS = 8
TOK = 128
WIN = 512
FEAT = PER * D
NX, NY, NZ, NC = 4, 4, 16, 2
PLANE = NY * NC
ROWS = PLANE * DOCS
COLS = NZ * DOCS
INV_TEMP = 50.0
SCALE2 = D ** (-0.5) * math.log2(math.e)

NEAR = (1, -1, 2, -2)
FAR = (5, -5)
FORWARD = {5: (3, 2, -2, 1, -1), -5: (-2, 2, -1, 1)}


def split2(a):
    hi = a.astype(BF16)
    return hi, (a - hi.astype(F32)).astype(BF16)


def kernel(
    lens, pair, q_hbm, k_hbm, v_hbm, emb_out, grad_out,
    qv, kb, vb, bias, pst, mst, lst, wo, wi, pooled, ucol, urow, prow,
    dsend, drecv, ssend, scol, rsend, srow, gsend, grecv, norms,
    lsem, k_s, k_r, v_s, v_r, w_s, w_r, p_s, p_r, u_s, u_r, c_s, c_r, d_s, d_r, t_s, t_r, a_s, a_r, g_s, g_r,
):
    dp = lax.axis_index("dp")
    x = lax.axis_index("sp")
    c = lax.rem(dp, NC)
    z = lax.rem(dp // NC, NZ)
    y = dp // (NC * NZ)
    mine = y * NC + c

    def at_x(d):
        return (dp, lax.rem(x + d, NX))

    def at_z(o):
        return ((y * NZ + lax.rem(z + o + NZ, NZ)) * NC + c, x)

    def at_plane(k):
        there_y, there_c = lax.rem(y + k // NC, NY), lax.rem(c + k % NC, NC)
        return ((there_y * NZ + z) * NC + there_c, x)

    def slot_to(k):
        return lax.rem(y + k // NC, NY) * NC + lax.rem(c + k % NC, NC)

    def slot_from(k):
        return lax.rem(y - k // NC + NY, NY) * NC + lax.rem(c + k % NC, NC)

    def z_from(o):
        return lax.rem(z - o + NZ, NZ)

    def x_from(d):
        return lax.rem(x - d + NX, NX)

    def copy(src, dst, ss, rs, there):
        return pltpu.make_async_remote_copy(
            src_ref=src, dst_ref=dst, send_sem=ss, recv_sem=rs, device_id=there, device_id_type=MESH
        )

    barrier = pltpu.get_barrier_semaphore()
    for d in range(1, NX):
        pl.semaphore_signal(barrier, inc=1, device_id=at_x(d), device_id_type=MESH)
    for k in range(1, PLANE):
        pl.semaphore_signal(barrier, inc=1, device_id=at_plane(k), device_id_type=MESH)
    for o in range(1, NZ):
        pl.semaphore_signal(barrier, inc=1, device_id=at_z(o), device_id_type=MESH)

    q_in = pltpu.make_async_copy(q_hbm, qv, lsem.at[0])
    k_in = pltpu.make_async_copy(k_hbm, kb.at[x], lsem.at[1])
    v_in = pltpu.make_async_copy(v_hbm.at[:, pl.ds(pl.multiple_of(x * D, D), D)], vb.at[x], lsem.at[2])
    k_in.start()
    q_in.start()
    v_in.start()

    ends = []
    total = 0
    for i in range(DOCS):
        total = total + lens[0, i]
        ends.append(total)

    def segment(places):
        out = jnp.zeros(places.shape, jnp.int32)
        for end in ends:
            out = out + (places >= end).astype(jnp.int32)
        return out

    def iota(shape, axis):
        return lax.broadcasted_iota(jnp.int32, shape, axis)

    q_segment = segment(x * TOK + iota((TOK, TOK), 1))
    row8 = iota((DOCS, D), 0)
    length = jnp.zeros((DOCS, D), F32)
    partner = jnp.zeros((DOCS, D), F32)
    for i in range(DOCS):
        length = jnp.where(row8 == i, lens[0, i].astype(F32), length)
        partner = jnp.where(row8 == i, pair[i].astype(F32), partner)
    prow[mine] = partner
    mst[...] = jnp.zeros_like(mst)
    lst[...] = jnp.ones_like(lst)

    def scores(e):
        block = x_from(e)
        k_segment = segment(block * TOK + iota((TOK, TOK), 0))
        bias[...] = jnp.where(k_segment == q_segment, 0.0, -1e30).astype(F32)

        def group(g, carry):
            key = kb[block, :, pl.ds(pl.multiple_of(g * D, D), D)]
            for j in range(PER):
                query = qv[:, pl.ds(pl.multiple_of((g * PER + j) * D, D), D)]
                s = lax.dot_general(key, query, NT, preferred_element_type=F32) * SCALE2 + bias[...]
                m = jnp.max(s, axis=0, keepdims=True)
                p = jnp.exp2(s - m)
                pst[e, g * PER + j] = p.astype(BF16)
                mst[e, g, j : j + 1, :] = m
                lst[e, g, j : j + 1, :] = jnp.sum(p, axis=0, keepdims=True)
            return carry

        lax.fori_loop(0, GROUPS, group, 0)

    k_in.wait()
    q_in.wait()
    v_in.wait()
    scores(0)

    pl.semaphore_wait(barrier, NX - 1 + PLANE - 1 + NZ - 1)

    k_copies = {d: copy(k_hbm, kb.at[x], k_s.at[d], k_r.at[d], at_x(d)) for d in (1, 3, 2)}
    v_copies = {}
    p_copies = {}
    for d in k_copies:
        k_copies[d].start()
    for d in (1, 3, 2):
        there = lax.rem(x + d, NX)
        v_copies[d] = copy(
            v_hbm.at[:, pl.ds(pl.multiple_of(there * D, D), D)], vb.at[x], v_s.at[d], v_r.at[d], at_x(d)
        )
        v_copies[d].start()
    for k in range(1, PLANE):
        p_copies[k] = copy(prow.at[mine], prow.at[mine], p_s.at[k], p_r.at[k], at_plane(k))
        p_copies[k].start()

    for d in (1, 3, 2):
        k_copies[d].wait_recv()
        scores(d)

    row16 = lax.rem(iota((2 * DOCS, TOK), 0), DOCS)

    def weigh(g, carry):
        ms = [mst[e, g] for e in range(NX)]
        top = functools.reduce(jnp.maximum, ms)
        fs = [jnp.exp2(m - top) for m in ms]
        inv = 1.0 / sum(lst[e, g] * fs[e] for e in range(NX))
        for e in range(NX):
            f = fs[e] * inv
            hi = f.astype(BF16).astype(F32)
            both = jnp.concatenate([hi, f - hi], axis=0)
            acc = jnp.zeros((2 * DOCS, TOK), F32)
            for j in range(PER):
                one = jnp.where(row16 == j, both, 0.0).astype(BF16)
                acc = acc + lax.dot_general(one, pst[e, g * PER + j], NT, preferred_element_type=F32)
            wo[g, :, pl.ds(pl.multiple_of(x_from(e) * TOK, TOK), TOK)] = acc[:DOCS] + acc[DOCS:]
        return carry

    lax.fori_loop(0, GROUPS, weigh, 0)

    w_copies = {
        d: copy(wo.at[lax.rem(x + d, NX)], wi.at[x], w_s.at[d], w_r.at[d], at_x(d)) for d in (2, 1, 3)
    }
    for d in w_copies:
        w_copies[d].start()
    onehot = (segment(iota((DOCS, WIN), 1)) == iota((DOCS, WIN), 0)).astype(F32)
    for d in (1, 3, 2):
        v_copies[d].wait_recv()
    weights = wo[x]
    for d in (1, 3, 2):
        w_copies[d].wait_recv()
        weights = weights + wi[x_from(d)]
    lhs = jnp.concatenate([weights[j : j + 1] * onehot for j in range(PER)], axis=0)
    hi, lo = split2(lhs)
    value = vb[...].reshape(WIN, D)
    sums = jnp.dot(hi, value, preferred_element_type=F32) + jnp.dot(lo, value, preferred_element_type=F32)
    for j in range(PER):
        pooled[:, j * D : (j + 1) * D] = sums[j * DOCS : (j + 1) * DOCS] / length
    short = pooled[...].astype(BF16)
    ucol[z] = short
    urow[mine] = short

    c_copies = {}
    u_copies = {}

    def send_col(origin, step, offset):
        c_copies[offset] = copy(ucol.at[origin], ucol.at[origin], c_s.at[offset % NZ], c_r.at[offset % NZ], at_z(step))
        c_copies[offset].start()

    for o in FAR + NEAR:
        send_col(z, o, o)
    for k in range(1, PLANE):
        u_copies[k] = copy(urow.at[mine], urow.at[mine], u_s.at[k], u_r.at[k], at_plane(k))
        u_copies[k].start()
    for o in FAR:
        c_copies[o].wait_recv()
        for step in FORWARD[o]:
            send_col(z_from(o), step, o + step)
    for k in range(1, PLANE):
        u_copies[k].wait_recv()
    for o in c_copies:
        if o not in FAR:
            c_copies[o].wait_recv()

    rows = urow[...].reshape(ROWS, FEAT)
    cols = ucol[...].reshape(COLS, FEAT)

    def squares(a):
        wide = a.astype(F32)
        hi, lo = split2(wide * wide)
        ones = jnp.ones((2 * DOCS, FEAT), BF16)
        return (
            lax.dot_general(ones, hi, NT, preferred_element_type=F32)
            + lax.dot_general(ones, lo, NT, preferred_element_type=F32)
        )[:DOCS]

    dsend[:ROWS, :] = lax.dot_general(rows, cols, NT, preferred_element_type=F32)
    dsend[ROWS:, :] = jnp.where(row8 == 0, squares(cols), squares(jnp.concatenate([rows, rows], axis=0)))
    d_copies = {d: copy(dsend, drecv.at[x], d_s.at[d], d_r.at[d], at_x(d)) for d in (2, 1, 3)}
    for d in d_copies:
        d_copies[d].start()
    for d in (1, 3, 2):
        d_copies[d].wait_recv()
    full = dsend[...]
    for d in range(1, NX):
        full = full + drecv[x_from(d)]

    r_id, c_id = iota((ROWS, COLS), 0), iota((ROWS, COLS), 1)
    eye = r_id == c_id

    def to_column(row):
        return jnp.sum(jnp.where(eye, row, 0.0), axis=1, keepdims=True)

    radius = jnp.sqrt(to_column(full[ROWS + 1 : ROWS + 2]) + 1e-6)
    norms[...] = jnp.broadcast_to(radius, (ROWS, D))
    inv_cols = 1.0 / jnp.sqrt(full[ROWS : ROWS + 1] + 1e-6)
    logits = full[:ROWS] * ((1.0 / radius) * (inv_cols * INV_TEMP))
    r_plane, r_doc = r_id // DOCS, lax.rem(r_id, DOCS)
    c_z, c_doc = c_id // DOCS, lax.rem(c_id, DOCS)
    same = (r_plane == mine) & (c_z == z) & (r_doc == c_doc)
    weight = jnp.where(same, 0.0, jnp.exp(logits))
    col_sum = jnp.sum(weight, axis=0, keepdims=True)
    row_sum = jnp.sum(jnp.where(eye, jnp.sum(weight, axis=1, keepdims=True), 0.0), axis=0, keepdims=True)
    ssend[...] = jnp.broadcast_to(col_sum, (DOCS, D))
    rsend[...] = jnp.broadcast_to(row_sum, (DOCS, D))
    t_copies = {}
    a_copies = {}
    for o in (8, 7, -7, 6, -6, 5, -5, 4, -4, 3, -3, 2, -2, 1, -1):
        t_copies[o] = copy(ssend.at[pl.ds(0, 1)], scol.at[z, pl.ds(0, 1)], t_s.at[o % NZ], t_r.at[o % NZ], at_z(o))
        t_copies[o].start()
    for k in range(1, PLANE):
        a_copies[k] = copy(rsend.at[pl.ds(0, 1)], srow.at[mine, pl.ds(0, 1)], a_s.at[k], a_r.at[k], at_plane(k))
        a_copies[k].start()

    own_radius = norms[pl.ds(pl.multiple_of(mine * DOCS, DOCS), DOCS), :]
    for j in range(PER):
        at = slice(j * D, (j + 1) * D)
        emb_out[:, at] = (pooled[:, at] / own_radius).astype(BF16)
    partners = prow_wait(p_copies, prow).reshape(ROWS, D)
    column_doc = ((y * NZ + c_z) * NC + c) * DOCS + c_doc
    pairs = jnp.where(partners == column_doc.astype(F32), 2.0, 0.0)
    for k in range(1, PLANE):
        a_copies[k].wait_recv()
        row_sum = row_sum + srow[slot_from(k), 0:1, :]
    for o in t_copies:
        t_copies[o].wait_recv()
        col_sum = col_sum + scol[z_from(o), 0:1, :]
    coef = weight * (1.0 / to_column(row_sum) + 1.0 / col_sum) - pairs
    along = jnp.sum(coef * logits, axis=1, keepdims=True)
    scaled = coef * (inv_cols * INV_TEMP)
    hi = scaled.astype(BF16)
    rest = scaled - hi.astype(F32)
    mid, lo = split2(rest)
    piece = (
        jnp.dot(hi, cols, preferred_element_type=F32)
        + jnp.dot(mid, cols, preferred_element_type=F32)
        + jnp.dot(lo, cols, preferred_element_type=F32)
    )
    gsend[:, :, :FEAT] = piece.reshape(PLANE, DOCS, FEAT)
    gsend[:, :, FEAT:] = jnp.broadcast_to(along, (ROWS, D)).reshape(PLANE, DOCS, D)
    g_copies = {}
    for k in range(PLANE - 1, 0, -1):
        g_copies[k] = copy(gsend.at[slot_to(k)], grecv.at[mine], g_s.at[k], g_r.at[k], at_plane(k))
        g_copies[k].start()
    gradient = gsend[mine]
    for k in range(1, PLANE):
        g_copies[k].wait_recv()
        gradient = gradient + grecv[slot_from(k)]
    projection = gradient[:, FEAT:]
    for j in range(PER):
        at = slice(j * D, (j + 1) * D)
        own = emb_out[:, at].astype(F32)
        grad_out[:, at] = (gradient[:, at] - own * projection) / own_radius

    for copies in (k_copies, v_copies, p_copies, w_copies, c_copies, u_copies, d_copies, t_copies, a_copies, g_copies):
        for key in copies:
            copies[key].wait_send()


def prow_wait(p_copies, prow):
    for k in p_copies:
        p_copies[k].wait_recv()
    return prow[...]


def per_device(queries, keys, values, document_lengths, pair_ids):
    dma = pltpu.SemaphoreType.DMA
    vmem = pl.BlockSpec(memory_space=pltpu.VMEM)
    smem = pl.BlockSpec(memory_space=pltpu.SMEM)
    hbm = pl.BlockSpec(memory_space=pl.ANY)
    return pl.pallas_call(
        kernel,
        out_shape=(jax.ShapeDtypeStruct((DOCS, FEAT), BF16), jax.ShapeDtypeStruct((DOCS, FEAT), F32)),
        in_specs=[smem, smem, hbm, hbm, hbm],
        out_specs=(vmem, vmem),
        scratch_shapes=[
            pltpu.VMEM((TOK, HEADS * D), BF16),
            pltpu.VMEM((NX, TOK, GROUPS * D), BF16),
            pltpu.VMEM((NX, TOK, D), BF16),
            pltpu.VMEM((TOK, TOK), F32),
            pltpu.VMEM((NX, HEADS, TOK, TOK), BF16),
            pltpu.VMEM((NX, GROUPS, DOCS, TOK), F32),
            pltpu.VMEM((NX, GROUPS, DOCS, TOK), F32),
            pltpu.VMEM((GROUPS, DOCS, WIN), F32),
            pltpu.VMEM((NX, DOCS, WIN), F32),
            pltpu.VMEM((DOCS, FEAT), F32),
            pltpu.VMEM((NZ, DOCS, FEAT), BF16),
            pltpu.VMEM((PLANE, DOCS, FEAT), BF16),
            pltpu.VMEM((PLANE, DOCS, D), F32),
            pltpu.VMEM((ROWS + DOCS, COLS), F32),
            pltpu.VMEM((NX, ROWS + DOCS, COLS), F32),
            pltpu.VMEM((DOCS, D), F32),
            pltpu.VMEM((NZ, DOCS, D), F32),
            pltpu.VMEM((DOCS, D), F32),
            pltpu.VMEM((PLANE, DOCS, D), F32),
            pltpu.VMEM((PLANE, DOCS, FEAT + D), F32),
            pltpu.VMEM((PLANE, DOCS, FEAT + D), F32),
            pltpu.VMEM((ROWS, D), F32),
            dma((3,)),
            dma((NX,)), dma((NX,)),
            dma((NX,)), dma((NX,)),
            dma((NX,)), dma((NX,)),
            dma((PLANE,)), dma((PLANE,)),
            dma((PLANE,)), dma((PLANE,)),
            dma((NZ,)), dma((NZ,)),
            dma((NX,)), dma((NX,)),
            dma((NZ,)), dma((NZ,)),
            dma((PLANE,)), dma((PLANE,)),
            dma((PLANE,)), dma((PLANE,)),
        ],
        compiler_params=pltpu.CompilerParams(
            collective_id=0, has_side_effects=True, vmem_limit_bytes=32 << 20
        ),
    )(document_lengths, pair_ids, queries, keys, values)


def solution(mesh):
    return jax.shard_map(
        per_device,
        mesh=mesh,
        in_specs=(
            P(("dp", "sp"), None),
            P(("dp", "sp"), None),
            P(("dp", "sp"), None),
            P("dp", None),
            P("dp"),
        ),
        out_specs=(P("dp", "sp"), P("dp", "sp")),
        check_vma=False,
    )
```

```python
import functools
import math

import jax
import jax.numpy as jnp
from jax import lax
from jax.experimental import pallas as pl
from jax.experimental.pallas import tpu as pltpu
from jax.sharding import PartitionSpec as P

MESH = pl.DeviceIdType.MESH
F32 = jnp.float32
BF16 = jnp.bfloat16
NT = (((1,), (1,)), ((), ()))

GROUPS = 4
PER = 7
HEADS = GROUPS * PER
D = 128
DOCS = 8
TOK = 128
WIN = 512
FEAT = PER * D
NX, NY, NZ, NC = 4, 4, 16, 2
PLANE = NY * NC
ROWS = PLANE * DOCS
COLS = NZ * DOCS
INV_TEMP = 50.0
SCALE2 = D ** (-0.5) * math.log2(math.e)

NEAR = (1, -1, 2, -2)
FAR = (5, -5)
FORWARD = {5: (3, 2, -2, 1, -1), -5: (-2, 2, -1, 1)}


def split2(a):
    hi = a.astype(BF16)
    return hi, (a - hi.astype(F32)).astype(BF16)


def kernel(
    lens_hbm, pair_hbm, q_hbm, k_hbm, v_hbm, out,
    lens, pair, qv, kb, vb, bias, pst, mst, lst, wo, wi, pooled, ucol, urow, prow,
    dsend, drecv, ssend, scol, rsend, srow, gsend, grecv, norms,
    lsem, k_s, k_r, v_s, v_r, w_s, w_r, p_s, p_r, u_s, u_r, c_s, c_r, d_s, d_r, t_s, t_r, a_s, a_r, g_s, g_r,
):
    dp = lax.axis_index("dp")
    x = lax.axis_index("sp")
    c = lax.rem(dp, NC)
    z = lax.rem(dp // NC, NZ)
    y = dp // (NC * NZ)
    mine = y * NC + c

    def at_x(d):
        return (dp, lax.rem(x + d, NX))

    def at_z(o):
        return ((y * NZ + lax.rem(z + o + NZ, NZ)) * NC + c, x)

    def at_plane(k):
        there_y, there_c = lax.rem(y + k // NC, NY), lax.rem(c + k % NC, NC)
        return ((there_y * NZ + z) * NC + there_c, x)

    def slot_to(k):
        return lax.rem(y + k // NC, NY) * NC + lax.rem(c + k % NC, NC)

    def slot_from(k):
        return lax.rem(y - k // NC + NY, NY) * NC + lax.rem(c + k % NC, NC)

    def z_from(o):
        return lax.rem(z - o + NZ, NZ)

    def x_from(d):
        return lax.rem(x - d + NX, NX)

    def copy(src, dst, ss, rs, there):
        return pltpu.make_async_remote_copy(
            src_ref=src, dst_ref=dst, send_sem=ss, recv_sem=rs, device_id=there, device_id_type=MESH
        )

    barrier = pltpu.get_barrier_semaphore()
    for d in range(1, NX):
        pl.semaphore_signal(barrier, inc=1, device_id=at_x(d), device_id_type=MESH)
    for k in range(1, PLANE):
        pl.semaphore_signal(barrier, inc=1, device_id=at_plane(k), device_id_type=MESH)
    for o in range(1, NZ):
        pl.semaphore_signal(barrier, inc=1, device_id=at_z(o), device_id_type=MESH)

    lens_in = pltpu.make_async_copy(lens_hbm, lens, lsem.at[0])
    pair_in = pltpu.make_async_copy(pair_hbm, pair, lsem.at[1])
    q_in = pltpu.make_async_copy(q_hbm, qv, lsem.at[2])
    v_in = pltpu.make_async_copy(v_hbm.at[:, pl.ds(pl.multiple_of(x * D, D), D)], vb.at[x], lsem.at[3])
    k_in = [
        pltpu.make_async_copy(k_hbm.at[:, g * D : (g + 1) * D], kb.at[g, x], lsem.at[4 + g]) for g in range(GROUPS)
    ]
    lens_in.start()
    pair_in.start()
    for one in k_in:
        one.start()
    q_in.start()
    v_in.start()
    lens_in.wait()
    pair_in.wait()

    ends = []
    total = 0
    for i in range(DOCS):
        total = total + lens[0, i]
        ends.append(total)

    def segment(places):
        out = jnp.zeros(places.shape, jnp.int32)
        for end in ends:
            out = out + (places >= end).astype(jnp.int32)
        return out

    def iota(shape, axis):
        return lax.broadcasted_iota(jnp.int32, shape, axis)

    q_segment = segment(x * TOK + iota((TOK, TOK), 1))
    row8 = iota((DOCS, D), 0)
    length = jnp.zeros((DOCS, D), F32)
    partner = jnp.zeros((DOCS, D), F32)
    for i in range(DOCS):
        length = jnp.where(row8 == i, lens[0, i].astype(F32), length)
        partner = jnp.where(row8 == i, pair[i].astype(F32), partner)
    prow[mine] = partner
    mst[...] = jnp.zeros_like(mst)
    lst[...] = jnp.ones_like(lst)

    for e in range(NX):
        k_segment = segment(x_from(e) * TOK + iota((TOK, TOK), 0))
        bias[e] = jnp.where(k_segment == q_segment, 0.0, -1e30).astype(F32)

    def scores(e, g):
        key = kb[g, x_from(e)]
        for j in range(PER):
            query = qv[:, pl.ds(pl.multiple_of((g * PER + j) * D, D), D)]
            s = lax.dot_general(key, query, NT, preferred_element_type=F32) * SCALE2 + bias[e]
            m = jnp.max(s, axis=0, keepdims=True)
            p = jnp.exp2(s - m)
            pst[e, g, :, j * TOK : (j + 1) * TOK] = p.astype(BF16)
            mst[e, g, j : j + 1, :] = m
            lst[e, g, j : j + 1, :] = jnp.sum(p, axis=0, keepdims=True)

    for one in k_in:
        one.wait()
    pl.semaphore_wait(barrier, NX - 1 + PLANE - 1 + NZ - 1)

    k_copies = {}
    v_copies = {}
    p_copies = {}
    w_copies = {}
    for i in range(GROUPS):
        for d in (1, 3, 2):
            g = lax.rem(x + d + 1 + i, GROUPS)
            k_copies[d, i] = copy(kb.at[g, x], kb.at[g, x], k_s.at[d, i], k_r.at[d, i], at_x(d))
            k_copies[d, i].start()
    for d in (1, 3, 2):
        there = lax.rem(x + d, NX)
        v_copies[d] = copy(
            v_hbm.at[:, pl.ds(pl.multiple_of(there * D, D), D)], vb.at[x], v_s.at[d], v_r.at[d], at_x(d)
        )
        v_copies[d].start()
    for k in range(1, PLANE):
        p_copies[k] = copy(prow.at[mine], prow.at[mine], p_s.at[k], p_r.at[k], at_plane(k))
        p_copies[k].start()
    q_in.wait()
    v_in.wait()

    def own(g, carry):
        scores(0, g)
        return carry

    lax.fori_loop(0, GROUPS, own, 0)

    row16 = lax.rem(iota((2 * DOCS, TOK), 0), DOCS)

    def weigh(g):
        ms = [mst[e, g] for e in range(NX)]
        top = functools.reduce(jnp.maximum, ms)
        fs = [jnp.exp2(m - top) for m in ms]
        inv = 1.0 / sum(lst[e, g] * fs[e] for e in range(NX))
        for e in range(NX):
            f = fs[e] * inv
            hi = f.astype(BF16).astype(F32)
            both = jnp.concatenate([hi, f - hi], axis=0)
            lhs = jnp.concatenate([jnp.where(row16 == j, both, 0.0).astype(BF16) for j in range(PER)], axis=1)
            acc = lax.dot_general(lhs, pst[e, g], NT, preferred_element_type=F32)
            wo[g, :, pl.ds(pl.multiple_of(x_from(e) * TOK, TOK), TOK)] = acc[:DOCS] + acc[DOCS:]

    for i in range(GROUPS):
        group = lax.rem(x + 1 + i, GROUPS)
        for d in (1, 3, 2):
            k_copies[d, i].wait_recv()
            scores(d, group)
        weigh(group)
        if i < GROUPS - 1:
            w_copies[i + 1] = copy(wo.at[group], wi.at[x], w_s.at[i + 1], w_r.at[i + 1], at_x(i + 1))
            w_copies[i + 1].start()
    onehot = (segment(iota((DOCS, WIN), 1)) == iota((DOCS, WIN), 0)).astype(F32)
    for d in (1, 3, 2):
        v_copies[d].wait_recv()
    weights = wo[x]
    for d in (1, 3, 2):
        w_copies[d].wait_recv()
        weights = weights + wi[x_from(d)]
    lhs = jnp.concatenate([weights[j : j + 1] * onehot for j in range(PER)], axis=0)
    hi, lo = split2(lhs)
    value = vb[...].reshape(WIN, D)
    sums = jnp.dot(hi, value, preferred_element_type=F32) + jnp.dot(lo, value, preferred_element_type=F32)
    for j in range(PER):
        pooled[:, j * D : (j + 1) * D] = sums[j * DOCS : (j + 1) * DOCS] / length
    short = pooled[...].astype(BF16)
    ucol[z] = short
    urow[mine] = short

    c_copies = {}
    u_copies = {}

    def send_col(origin, step, offset):
        c_copies[offset] = copy(ucol.at[origin], ucol.at[origin], c_s.at[offset % NZ], c_r.at[offset % NZ], at_z(step))
        c_copies[offset].start()

    for o in FAR + NEAR:
        send_col(z, o, o)
    for k in range(1, PLANE):
        u_copies[k] = copy(urow.at[mine], urow.at[mine], u_s.at[k], u_r.at[k], at_plane(k))
        u_copies[k].start()
    for o in FAR:
        c_copies[o].wait_recv()
        for step in FORWARD[o]:
            send_col(z_from(o), step, o + step)
    for k in range(1, PLANE):
        u_copies[k].wait_recv()
    for o in c_copies:
        if o not in FAR:
            c_copies[o].wait_recv()

    rows = urow[...].reshape(ROWS, FEAT)
    cols = ucol[...].reshape(COLS, FEAT)

    def squares(a):
        wide = a.astype(F32)
        hi, lo = split2(wide * wide)
        ones = jnp.ones((2 * DOCS, FEAT), BF16)
        return (
            lax.dot_general(ones, hi, NT, preferred_element_type=F32)
            + lax.dot_general(ones, lo, NT, preferred_element_type=F32)
        )[:DOCS]

    dsend[:ROWS, :] = lax.dot_general(rows, cols, NT, preferred_element_type=F32)
    dsend[ROWS:, :] = jnp.where(row8 == 0, squares(cols), squares(jnp.concatenate([rows, rows], axis=0)))
    d_copies = {d: copy(dsend, drecv.at[x], d_s.at[d], d_r.at[d], at_x(d)) for d in (2, 1, 3)}
    for d in d_copies:
        d_copies[d].start()
    for d in (1, 3, 2):
        d_copies[d].wait_recv()
    full = dsend[...]
    for d in range(1, NX):
        full = full + drecv[x_from(d)]

    r_id, c_id = iota((ROWS, COLS), 0), iota((ROWS, COLS), 1)
    eye = r_id == c_id

    def to_column(row):
        return jnp.sum(jnp.where(eye, row, 0.0), axis=1, keepdims=True)

    radius = jnp.sqrt(to_column(full[ROWS + 1 : ROWS + 2]) + 1e-6)
    norms[...] = jnp.broadcast_to(radius, (ROWS, D))
    inv_cols = 1.0 / jnp.sqrt(full[ROWS : ROWS + 1] + 1e-6)
    logits = full[:ROWS] * ((1.0 / radius) * (inv_cols * INV_TEMP))
    r_plane, r_doc = r_id // DOCS, lax.rem(r_id, DOCS)
    c_z, c_doc = c_id // DOCS, lax.rem(c_id, DOCS)
    same = (r_plane == mine) & (c_z == z) & (r_doc == c_doc)
    weight = jnp.where(same, 0.0, jnp.exp(logits))
    col_sum = jnp.sum(weight, axis=0, keepdims=True)
    row_sum = jnp.sum(jnp.where(eye, jnp.sum(weight, axis=1, keepdims=True), 0.0), axis=0, keepdims=True)
    ssend[...] = jnp.broadcast_to(col_sum, (DOCS, D))
    rsend[...] = jnp.broadcast_to(row_sum, (DOCS, D))
    t_copies = {}
    a_copies = {}
    for o in (8, 7, -7, 6, -6, 5, -5, 4, -4, 3, -3, 2, -2, 1, -1):
        t_copies[o] = copy(ssend.at[pl.ds(0, 1)], scol.at[z, pl.ds(0, 1)], t_s.at[o % NZ], t_r.at[o % NZ], at_z(o))
        t_copies[o].start()
    for k in range(1, PLANE):
        a_copies[k] = copy(rsend.at[pl.ds(0, 1)], srow.at[mine, pl.ds(0, 1)], a_s.at[k], a_r.at[k], at_plane(k))
        a_copies[k].start()

    own_radius = norms[pl.ds(pl.multiple_of(mine * DOCS, DOCS), DOCS), :]
    for j in range(PER):
        at = slice(j * D, (j + 1) * D)
        out[:, at] = (pooled[:, at] / own_radius).astype(BF16).astype(F32)
    partners = prow_wait(p_copies, prow).reshape(ROWS, D)
    column_doc = ((y * NZ + c_z) * NC + c) * DOCS + c_doc
    pairs = jnp.where(partners == column_doc.astype(F32), 2.0, 0.0)
    for k in range(1, PLANE):
        a_copies[k].wait_recv()
        row_sum = row_sum + srow[slot_from(k), 0:1, :]
    for o in t_copies:
        t_copies[o].wait_recv()
        col_sum = col_sum + scol[z_from(o), 0:1, :]
    coef = weight * (1.0 / to_column(row_sum) + 1.0 / col_sum) - pairs
    along = jnp.sum(coef * logits, axis=1, keepdims=True)
    scaled = coef * (inv_cols * INV_TEMP)
    hi = scaled.astype(BF16)
    rest = scaled - hi.astype(F32)
    mid, lo = split2(rest)
    piece = (
        jnp.dot(hi, cols, preferred_element_type=F32)
        + jnp.dot(mid, cols, preferred_element_type=F32)
        + jnp.dot(lo, cols, preferred_element_type=F32)
    )
    high, low = split2(along)
    first = iota((ROWS, D), 1) < D // 2
    sides = jnp.where(first, high.astype(F32), low.astype(F32)).astype(BF16)
    gsend[:, :, :FEAT] = piece.astype(BF16).reshape(PLANE, DOCS, FEAT)
    gsend[:, :, FEAT:] = sides.reshape(PLANE, DOCS, D)
    g_copies = {}
    for k in range(PLANE - 1, 0, -1):
        g_copies[k] = copy(gsend.at[slot_to(k)], grecv.at[mine], g_s.at[k], g_r.at[k], at_plane(k))
        g_copies[k].start()
    gradient = gsend[mine].astype(F32)
    for k in range(1, PLANE):
        g_copies[k].wait_recv()
        gradient = gradient + grecv[slot_from(k)].astype(F32)
    tail = gradient[:, FEAT:]
    projection = tail[:, :1] + tail[:, D // 2 : D // 2 + 1]
    for j in range(PER):
        at = slice(j * D, (j + 1) * D)
        out[:, FEAT + j * D : FEAT + (j + 1) * D] = (gradient[:, at] - out[:, at] * projection) / own_radius

    for copies in (
        k_copies, v_copies, p_copies, w_copies, c_copies, u_copies, d_copies, t_copies, a_copies, g_copies
    ):
        for key in copies:
            copies[key].wait_send()


def prow_wait(p_copies, prow):
    for k in p_copies:
        p_copies[k].wait_recv()
    return prow[...]


def per_device(queries, keys, values, document_lengths, pair_ids):
    dma = pltpu.SemaphoreType.DMA
    vmem = pl.BlockSpec(memory_space=pltpu.VMEM)
    hbm = pl.BlockSpec(memory_space=pl.ANY)
    both = pl.pallas_call(
        kernel,
        out_shape=jax.ShapeDtypeStruct((DOCS, 2 * FEAT), F32),
        in_specs=[hbm] * 5,
        out_specs=vmem,
        scratch_shapes=[
            pltpu.SMEM((1, DOCS), jnp.int32),
            pltpu.SMEM((DOCS,), jnp.int32),
            pltpu.VMEM((TOK, HEADS * D), BF16),
            pltpu.VMEM((GROUPS, NX, TOK, D), BF16),
            pltpu.VMEM((NX, TOK, D), BF16),
            pltpu.VMEM((NX, TOK, TOK), F32),
            pltpu.VMEM((NX, GROUPS, TOK, PER * TOK), BF16),
            pltpu.VMEM((NX, GROUPS, DOCS, TOK), F32),
            pltpu.VMEM((NX, GROUPS, DOCS, TOK), F32),
            pltpu.VMEM((GROUPS, DOCS, WIN), F32),
            pltpu.VMEM((NX, DOCS, WIN), F32),
            pltpu.VMEM((DOCS, FEAT), F32),
            pltpu.VMEM((NZ, DOCS, FEAT), BF16),
            pltpu.VMEM((PLANE, DOCS, FEAT), BF16),
            pltpu.VMEM((PLANE, DOCS, D), F32),
            pltpu.VMEM((ROWS + DOCS, COLS), F32),
            pltpu.VMEM((NX, ROWS + DOCS, COLS), F32),
            pltpu.VMEM((DOCS, D), F32),
            pltpu.VMEM((NZ, DOCS, D), F32),
            pltpu.VMEM((DOCS, D), F32),
            pltpu.VMEM((PLANE, DOCS, D), F32),
            pltpu.VMEM((PLANE, DOCS, FEAT + D), BF16),
            pltpu.VMEM((PLANE, DOCS, FEAT + D), BF16),
            pltpu.VMEM((ROWS, D), F32),
            dma((4 + GROUPS,)),
            dma((NX, GROUPS)), dma((NX, GROUPS)),
            dma((NX,)), dma((NX,)),
            dma((NX,)), dma((NX,)),
            dma((PLANE,)), dma((PLANE,)),
            dma((PLANE,)), dma((PLANE,)),
            dma((NZ,)), dma((NZ,)),
            dma((NX,)), dma((NX,)),
            dma((NZ,)), dma((NZ,)),
            dma((PLANE,)), dma((PLANE,)),
            dma((PLANE,)), dma((PLANE,)),
        ],
        compiler_params=pltpu.CompilerParams(
            collective_id=0, has_side_effects=True, vmem_limit_bytes=60 << 20
        ),
    )(document_lengths, pair_ids, queries, keys, values)
    return both[:, :FEAT].astype(BF16), both[:, FEAT:]


def solution(mesh):
    return jax.shard_map(
        per_device,
        mesh=mesh,
        in_specs=(
            P(("dp", "sp"), None),
            P(("dp", "sp"), None),
            P(("dp", "sp"), None),
            P("dp", None),
            P("dp"),
        ),
        out_specs=(P("dp", "sp"), P("dp", "sp")),
        check_vma=False,
    )
```

```python
import functools
import math

import jax
import jax.numpy as jnp
from jax import lax
from jax.experimental import pallas as pl
from jax.experimental.pallas import tpu as pltpu
from jax.sharding import PartitionSpec as P

MESH = pl.DeviceIdType.MESH
F32 = jnp.float32
BF16 = jnp.bfloat16
NT = (((1,), (1,)), ((), ()))

GROUPS = 4
PER = 7
HEADS = GROUPS * PER
D = 128
DOCS = 8
TOK = 128
WIN = 512
FEAT = PER * D
NX, NY, NZ, NC = 4, 4, 16, 2
PLANE = NY * NC
ROWS = PLANE * DOCS
COLS = NZ * DOCS
INV_TEMP = 50.0
SCALE2 = D ** (-0.5) * math.log2(math.e)

NEAR = (1, -1, 2, -2)
FAR = (5, -5)
FORWARD = {5: (2, -2, 1, -1), -5: (-2, 2, -1, 1)}


def split2(a):
    hi = a.astype(BF16)
    return hi, (a - hi.astype(F32)).astype(BF16)


def kernel(
    lens_hbm, pair_hbm, q_hbm, k_hbm, v_hbm, out,
    lens, pair, qv, kb, vb, bias, pst, mst, lst, wo, wi, pooled, ucol, urow, prow,
    dsend, drecv, ssend, scol, rsend, srow, gsend, grecv, norms,
    heard, lsem, k_s, k_r, v_s, v_r, w_s, w_r, p_s, p_r, u_s, u_r, c_s, c_r, d_s, d_r, t_s, t_r, a_s, a_r, g_s, g_r,
):
    dp = lax.axis_index("dp")
    x = lax.axis_index("sp")
    c = lax.rem(dp, NC)
    z = lax.rem(dp // NC, NZ)
    y = dp // (NC * NZ)
    mine = y * NC + c

    def at_x(d):
        return (dp, lax.rem(x + d, NX))

    def at_z(o):
        return ((y * NZ + lax.rem(z + o + NZ, NZ)) * NC + c, x)

    def at_plane(k):
        there_y, there_c = lax.rem(y + k // NC, NY), lax.rem(c + k % NC, NC)
        return ((there_y * NZ + z) * NC + there_c, x)

    def slot_to(k):
        return lax.rem(y + k // NC, NY) * NC + lax.rem(c + k % NC, NC)

    def slot_from(k):
        return lax.rem(y - k // NC + NY, NY) * NC + lax.rem(c + k % NC, NC)

    def z_from(o):
        return lax.rem(z - o + NZ, NZ)

    def x_from(d):
        return lax.rem(x - d + NX, NX)

    def copy(src, dst, ss, rs, there):
        return pltpu.make_async_remote_copy(
            src_ref=src, dst_ref=dst, send_sem=ss, recv_sem=rs, device_id=there, device_id_type=MESH
        )

    barrier = pltpu.get_barrier_semaphore()
    for d in range(1, NX):
        pl.semaphore_signal(barrier, inc=1, device_id=at_x(d), device_id_type=MESH)
    for k in range(1, PLANE):
        pl.semaphore_signal(barrier, inc=1, device_id=at_plane(k), device_id_type=MESH)
    for o in NEAR:
        pl.semaphore_signal(barrier, inc=1, device_id=at_z(o), device_id_type=MESH)

    lens_in = pltpu.make_async_copy(lens_hbm, lens, lsem.at[0])
    pair_in = pltpu.make_async_copy(pair_hbm, pair, lsem.at[1])
    q_in = pltpu.make_async_copy(q_hbm, qv, lsem.at[2])
    v_in = pltpu.make_async_copy(v_hbm.at[:, pl.ds(pl.multiple_of(x * D, D), D)], vb.at[x], lsem.at[3])
    k_in = [
        pltpu.make_async_copy(k_hbm.at[:, g * D : (g + 1) * D], kb.at[g, x], lsem.at[4 + g]) for g in range(GROUPS)
    ]
    for one in k_in:
        one.start()
    lens_in.start()
    pair_in.start()
    q_in.start()
    v_in.start()
    for one in k_in:
        one.wait()
    pl.semaphore_wait(barrier, NX - 1 + PLANE - 1 + len(NEAR))

    k_copies = {}
    v_copies = {}
    p_copies = {}
    w_copies = {}
    for i in range(GROUPS):
        for d in (1, 3, 2):
            g = lax.rem(x + d + 1 + i, GROUPS)
            k_copies[d, i] = copy(kb.at[g, x], kb.at[g, x], k_s.at[d, i], k_r.at[d, i], at_x(d))
            k_copies[d, i].start()
    for d in (1, 3, 2):
        there = lax.rem(x + d, NX)
        v_copies[d] = copy(
            v_hbm.at[:, pl.ds(pl.multiple_of(there * D, D), D)], vb.at[x], v_s.at[d], v_r.at[d], at_x(d)
        )
        v_copies[d].start()
    for o in (2, -2):
        pl.semaphore_signal(heard.at[0], inc=1, device_id=at_z(o), device_id_type=MESH)
    lens_in.wait()
    pair_in.wait()

    ends = []
    total = 0
    for i in range(DOCS):
        total = total + lens[0, i]
        ends.append(total)

    def segment(places):
        out = jnp.zeros(places.shape, jnp.int32)
        for end in ends:
            out = out + (places >= end).astype(jnp.int32)
        return out

    def iota(shape, axis):
        return lax.broadcasted_iota(jnp.int32, shape, axis)

    q_segment = segment(x * TOK + iota((TOK, TOK), 1))
    row8 = iota((DOCS, D), 0)
    length = jnp.zeros((DOCS, D), F32)
    partner = jnp.zeros((DOCS, D), F32)
    for i in range(DOCS):
        length = jnp.where(row8 == i, lens[0, i].astype(F32), length)
        partner = jnp.where(row8 == i, pair[i].astype(F32), partner)
    prow[mine] = partner
    mst[...] = jnp.zeros_like(mst)
    lst[...] = jnp.ones_like(lst)

    for e in range(NX):
        k_segment = segment(x_from(e) * TOK + iota((TOK, TOK), 0))
        bias[e] = jnp.where(k_segment == q_segment, 0.0, -1e30).astype(F32)

    def scores(e, g):
        key = kb[g, x_from(e)]
        for j in range(PER):
            query = qv[:, pl.ds(pl.multiple_of((g * PER + j) * D, D), D)]
            s = lax.dot_general(key, query, NT, preferred_element_type=F32) * SCALE2 + bias[e]
            m = jnp.max(s, axis=0, keepdims=True)
            p = jnp.exp2(s - m)
            pst[e, g, :, j * TOK : (j + 1) * TOK] = p.astype(BF16)
            mst[e, g, j : j + 1, :] = m
            lst[e, g, j : j + 1, :] = jnp.sum(p, axis=0, keepdims=True)

    for k in range(1, PLANE):
        p_copies[k] = copy(prow.at[mine], prow.at[mine], p_s.at[k], p_r.at[k], at_plane(k))
        p_copies[k].start()
    q_in.wait()
    v_in.wait()

    def own(g, carry):
        scores(0, g)
        return carry

    lax.fori_loop(0, GROUPS, own, 0)
    pl.semaphore_wait(heard.at[0], 2)
    for o in (4, -4):
        pl.semaphore_signal(heard.at[1], inc=1, device_id=at_z(o), device_id_type=MESH)

    row16 = lax.rem(iota((2 * DOCS, TOK), 0), DOCS)

    def weigh(g):
        ms = [mst[e, g] for e in range(NX)]
        top = functools.reduce(jnp.maximum, ms)
        fs = [jnp.exp2(m - top) for m in ms]
        inv = 1.0 / sum(lst[e, g] * fs[e] for e in range(NX))
        for e in range(NX):
            f = fs[e] * inv
            hi = f.astype(BF16).astype(F32)
            both = jnp.concatenate([hi, f - hi], axis=0)
            lhs = jnp.concatenate([jnp.where(row16 == j, both, 0.0).astype(BF16) for j in range(PER)], axis=1)
            acc = lax.dot_general(lhs, pst[e, g], NT, preferred_element_type=F32)
            wo[g, :, pl.ds(pl.multiple_of(x_from(e) * TOK, TOK), TOK)] = acc[:DOCS] + acc[DOCS:]

    def key_copy(d, i):
        g = lax.rem(x + d + 1 + i, GROUPS)
        return copy(kb.at[g, x], kb.at[g, x], k_s.at[d, i], k_r.at[d, i], at_x(d))

    def step(i, carry):
        group = lax.rem(x + 1 + i, GROUPS)

        def piece(t, inner):
            d = 1 + lax.rem(2 * t, NX - 1)
            key_copy(d, i).wait_recv()
            scores(d, group)
            return inner

        lax.fori_loop(0, NX - 1, piece, 0)
        weigh(group)

        @pl.when(i < GROUPS - 1)
        def _():
            copy(wo.at[group], wi.at[x], w_s.at[i + 1], w_r.at[i + 1], at_x(i + 1)).start()

        return carry

    lax.fori_loop(0, GROUPS, step, 0)
    pl.semaphore_wait(heard.at[1], 2)
    for d in range(1, NX):
        group = lax.rem(x + d, GROUPS)
        w_copies[d] = copy(wo.at[group], wi.at[x], w_s.at[d], w_r.at[d], at_x(d))
    onehot = (segment(iota((DOCS, WIN), 1)) == iota((DOCS, WIN), 0)).astype(F32)
    for d in (1, 3, 2):
        v_copies[d].wait_recv()
    weights = wo[x]
    for d in (1, 3, 2):
        w_copies[d].wait_recv()
        weights = weights + wi[x_from(d)]
    lhs = jnp.concatenate([weights[j : j + 1] * onehot for j in range(PER)], axis=0)
    hi, lo = split2(lhs)
    value = vb[...].reshape(WIN, D)
    sums = jnp.dot(hi, value, preferred_element_type=F32) + jnp.dot(lo, value, preferred_element_type=F32)
    for j in range(PER):
        pooled[:, j * D : (j + 1) * D] = sums[j * DOCS : (j + 1) * DOCS] / length
    short = pooled[...].astype(BF16)
    ucol[z] = short
    urow[mine] = short

    c_copies = {}
    u_copies = {}

    def send_col(origin, step, offset):
        c_copies[offset] = copy(ucol.at[origin], ucol.at[origin], c_s.at[offset % NZ], c_r.at[offset % NZ], at_z(step))
        c_copies[offset].start()

    for o in FAR + (8,) + NEAR:
        send_col(z, o, o)
    for k in range(1, PLANE):
        u_copies[k] = copy(urow.at[mine], urow.at[mine], u_s.at[k], u_r.at[k], at_plane(k))
        u_copies[k].start()
    for o in FAR:
        c_copies[o].wait_recv()
        for step in FORWARD[o]:
            send_col(z_from(o), step, o + step)
    for k in range(1, PLANE):
        u_copies[k].wait_recv()
    for o in c_copies:
        if o not in FAR:
            c_copies[o].wait_recv()

    rows = urow[...].reshape(ROWS, FEAT)
    cols = ucol[...].reshape(COLS, FEAT)

    def squares(a):
        wide = a.astype(F32)
        return jnp.sum(wide * wide, axis=1, keepdims=True)

    def to_row(column):
        n = column.shape[0]
        return jnp.sum(jnp.where(iota((n, D), 0) == iota((n, D), 1), column, 0.0), axis=0, keepdims=True)

    dsend[:ROWS, :] = lax.dot_general(rows, cols, NT, preferred_element_type=F32)
    dsend[ROWS:, :] = jnp.where(row8 == 0, to_row(squares(cols)), to_row(squares(rows)))
    d_copies = {d: copy(dsend, drecv.at[x], d_s.at[d], d_r.at[d], at_x(d)) for d in (2, 1, 3)}
    for d in d_copies:
        d_copies[d].start()
    for d in (1, 3, 2):
        d_copies[d].wait_recv()
    full = dsend[...]
    for d in range(1, NX):
        full = full + drecv[x_from(d)]

    r_id, c_id = iota((ROWS, COLS), 0), iota((ROWS, COLS), 1)
    eye = r_id == c_id

    def to_column(row):
        return jnp.sum(jnp.where(eye, row, 0.0), axis=1, keepdims=True)

    radius = jnp.sqrt(to_column(full[ROWS + 1 : ROWS + 2]) + 1e-6)
    norms[...] = jnp.broadcast_to(radius, (ROWS, D))
    inv_cols = 1.0 / jnp.sqrt(full[ROWS : ROWS + 1] + 1e-6)
    logits = full[:ROWS] * ((1.0 / radius) * (inv_cols * INV_TEMP))
    r_plane, r_doc = r_id // DOCS, lax.rem(r_id, DOCS)
    c_z, c_doc = c_id // DOCS, lax.rem(c_id, DOCS)
    same = (r_plane == mine) & (c_z == z) & (r_doc == c_doc)
    weight = jnp.where(same, 0.0, jnp.exp(logits))
    col_sum = jnp.sum(weight, axis=0, keepdims=True)
    row_sum = to_row(jnp.sum(weight, axis=1, keepdims=True))
    ssend[...] = jnp.broadcast_to(col_sum, (DOCS, D))
    rsend[...] = jnp.broadcast_to(row_sum, (DOCS, D))
    t_copies = {}
    a_copies = {}
    for o in (8, 7, -7, 6, -6, 5, -5, 4, -4, 3, -3, 2, -2, 1, -1):
        t_copies[o] = copy(ssend.at[pl.ds(0, 1)], scol.at[z, pl.ds(0, 1)], t_s.at[o % NZ], t_r.at[o % NZ], at_z(o))
        t_copies[o].start()
    for k in range(1, PLANE):
        a_copies[k] = copy(rsend.at[pl.ds(0, 1)], srow.at[mine, pl.ds(0, 1)], a_s.at[k], a_r.at[k], at_plane(k))
        a_copies[k].start()

    own_radius = norms[pl.ds(pl.multiple_of(mine * DOCS, DOCS), DOCS), :]
    for j in range(PER):
        at = slice(j * D, (j + 1) * D)
        out[:, at] = pooled[:, at] / own_radius
    partners = prow_wait(p_copies, prow).reshape(ROWS, D)
    column_doc = ((y * NZ + c_z) * NC + c) * DOCS + c_doc
    pairs = jnp.where(partners == column_doc.astype(F32), 2.0, 0.0)
    for k in range(1, PLANE):
        a_copies[k].wait_recv()
        row_sum = row_sum + srow[slot_from(k), 0:1, :]
    for o in t_copies:
        t_copies[o].wait_recv()
        col_sum = col_sum + scol[z_from(o), 0:1, :]
    coef = weight * (1.0 / to_column(row_sum) + 1.0 / col_sum) - pairs
    along = jnp.sum(coef * logits, axis=1, keepdims=True)
    scaled = coef * (inv_cols * INV_TEMP)
    hi = scaled.astype(BF16)
    rest = scaled - hi.astype(F32)
    mid, lo = split2(rest)
    piece = (
        jnp.dot(hi, cols, preferred_element_type=F32)
        + jnp.dot(mid, cols, preferred_element_type=F32)
        + jnp.dot(lo, cols, preferred_element_type=F32)
    )
    high, low = split2(along)
    first = iota((ROWS, D), 1) < D // 2
    sides = jnp.where(first, high.astype(F32), low.astype(F32)).astype(BF16)
    gsend[:, :, :FEAT] = piece.astype(BF16).reshape(PLANE, DOCS, FEAT)
    gsend[:, :, FEAT:] = sides.reshape(PLANE, DOCS, D)
    g_copies = {}
    for k in range(PLANE - 1, 0, -1):
        g_copies[k] = copy(gsend.at[slot_to(k)], grecv.at[mine], g_s.at[k], g_r.at[k], at_plane(k))
        g_copies[k].start()
    gradient = gsend[mine].astype(F32)
    for k in range(1, PLANE):
        g_copies[k].wait_recv()
        gradient = gradient + grecv[slot_from(k)].astype(F32)
    tail = gradient[:, FEAT:]
    projection = tail[:, :1] + tail[:, D // 2 : D // 2 + 1]
    for j in range(PER):
        out[:, FEAT + j * D : FEAT + (j + 1) * D] = gradient[:, j * D : (j + 1) * D] / own_radius
    out[:, 2 * FEAT :] = projection / own_radius

    for copies in (
        k_copies, v_copies, p_copies, w_copies, c_copies, u_copies, d_copies, t_copies, a_copies, g_copies
    ):
        for key in copies:
            copies[key].wait_send()


def prow_wait(p_copies, prow):
    for k in p_copies:
        p_copies[k].wait_recv()
    return prow[...]


def per_device(queries, keys, values, document_lengths, pair_ids):
    dma = pltpu.SemaphoreType.DMA
    vmem = pl.BlockSpec(memory_space=pltpu.VMEM)
    hbm = pl.BlockSpec(memory_space=pl.ANY)
    both = pl.pallas_call(
        kernel,
        out_shape=jax.ShapeDtypeStruct((DOCS, 2 * FEAT + D), F32),
        in_specs=[hbm] * 5,
        out_specs=vmem,
        scratch_shapes=[
            pltpu.SMEM((1, DOCS), jnp.int32),
            pltpu.SMEM((DOCS,), jnp.int32),
            pltpu.VMEM((TOK, HEADS * D), BF16),
            pltpu.VMEM((GROUPS, NX, TOK, D), BF16),
            pltpu.VMEM((NX, TOK, D), BF16),
            pltpu.VMEM((NX, TOK, TOK), F32),
            pltpu.VMEM((NX, GROUPS, TOK, PER * TOK), BF16),
            pltpu.VMEM((NX, GROUPS, DOCS, TOK), F32),
            pltpu.VMEM((NX, GROUPS, DOCS, TOK), F32),
            pltpu.VMEM((GROUPS, DOCS, WIN), F32),
            pltpu.VMEM((NX, DOCS, WIN), F32),
            pltpu.VMEM((DOCS, FEAT), F32),
            pltpu.VMEM((NZ, DOCS, FEAT), BF16),
            pltpu.VMEM((PLANE, DOCS, FEAT), BF16),
            pltpu.VMEM((PLANE, DOCS, D), F32),
            pltpu.VMEM((ROWS + DOCS, COLS), F32),
            pltpu.VMEM((NX, ROWS + DOCS, COLS), F32),
            pltpu.VMEM((DOCS, D), F32),
            pltpu.VMEM((NZ, DOCS, D), F32),
            pltpu.VMEM((DOCS, D), F32),
            pltpu.VMEM((PLANE, DOCS, D), F32),
            pltpu.VMEM((PLANE, DOCS, FEAT + D), BF16),
            pltpu.VMEM((PLANE, DOCS, FEAT + D), BF16),
            pltpu.VMEM((ROWS, D), F32),
            pltpu.SemaphoreType.REGULAR((2,)),
            dma((4 + GROUPS,)),
            dma((NX, GROUPS)), dma((NX, GROUPS)),
            dma((NX,)), dma((NX,)),
            dma((NX,)), dma((NX,)),
            dma((PLANE,)), dma((PLANE,)),
            dma((PLANE,)), dma((PLANE,)),
            dma((NZ,)), dma((NZ,)),
            dma((NX,)), dma((NX,)),
            dma((NZ,)), dma((NZ,)),
            dma((PLANE,)), dma((PLANE,)),
            dma((PLANE,)), dma((PLANE,)),
        ],
        compiler_params=pltpu.CompilerParams(
            collective_id=0, has_side_effects=True, vmem_limit_bytes=60 << 20
        ),
    )(document_lengths, pair_ids, queries, keys, values)
    embeddings = both[:, :FEAT].astype(BF16)
    grads = both[:, FEAT : 2 * FEAT] - embeddings.astype(F32) * both[:, 2 * FEAT : 2 * FEAT + 1]
    return embeddings, grads


def solution(mesh):
    return jax.shard_map(
        per_device,
        mesh=mesh,
        in_specs=(
            P(("dp", "sp"), None),
            P(("dp", "sp"), None),
            P(("dp", "sp"), None),
            P("dp", None),
            P("dp"),
        ),
        out_specs=(P("dp", "sp"), P("dp", "sp")),
        check_vma=False,
    )
```

```python
import functools
import math

import jax
import jax.numpy as jnp
from jax import lax
from jax.experimental import pallas as pl
from jax.experimental.pallas import tpu as pltpu
from jax.sharding import PartitionSpec as P

MESH = pl.DeviceIdType.MESH
F32 = jnp.float32
BF16 = jnp.bfloat16
NT = (((1,), (1,)), ((), ()))

GROUPS = 4
PER = 7
HEADS = GROUPS * PER
D = 128
DOCS = 8
TOK = 128
WIN = 512
FEAT = PER * D
NX, NY, NZ, NC = 4, 4, 16, 2
PLANE = NY * NC
ROWS = PLANE * DOCS
COLS = NZ * DOCS
INV_TEMP = 50.0
SCALE2 = D ** (-0.5) * math.log2(math.e)

NEAR = (1, -1, 2, -2)
FAR = (5, -5)
FORWARD = {5: (2, -2, 1, -1), -5: (-2, 2, -1, 1)}


def split2(a):
    hi = a.astype(BF16)
    return hi, (a - hi.astype(F32)).astype(BF16)


def kernel(
    lens_hbm, pair_hbm, q_hbm, k_hbm, v_hbm, out,
    lens, pair, qv, kb, vb, bias, pst, mst, lst, wo, wi, pooled, ucol, urow, prow,
    dsend, drecv, ssend, scol, rsend, srow, gsend, grecv, norms,
    heard, lsem, k_s, k_r, v_s, v_r, w_s, w_r, p_s, p_r, u_s, u_r, c_s, c_r, d_s, d_r, t_s, t_r, a_s, a_r, g_s, g_r,
):
    dp = lax.axis_index("dp")
    x = lax.axis_index("sp")
    c = lax.rem(dp, NC)
    z = lax.rem(dp // NC, NZ)
    y = dp // (NC * NZ)
    mine = y * NC + c

    def at_x(d):
        return (dp, lax.rem(x + d, NX))

    def at_z(o):
        return ((y * NZ + lax.rem(z + o + NZ, NZ)) * NC + c, x)

    def at_plane(k):
        there_y, there_c = lax.rem(y + k // NC, NY), lax.rem(c + k % NC, NC)
        return ((there_y * NZ + z) * NC + there_c, x)

    def slot_to(k):
        return lax.rem(y + k // NC, NY) * NC + lax.rem(c + k % NC, NC)

    def slot_from(k):
        return lax.rem(y - k // NC + NY, NY) * NC + lax.rem(c + k % NC, NC)

    def z_from(o):
        return lax.rem(z - o + NZ, NZ)

    def x_from(d):
        return lax.rem(x - d + NX, NX)

    def copy(src, dst, ss, rs, there):
        return pltpu.make_async_remote_copy(
            src_ref=src, dst_ref=dst, send_sem=ss, recv_sem=rs, device_id=there, device_id_type=MESH
        )

    near = [at_plane(1), at_plane(NC), at_plane((NY - 1) * NC), at_z(1), at_z(-1)]
    barrier = pltpu.get_barrier_semaphore()
    for d in (2, 1, 3):
        pl.semaphore_signal(barrier, inc=1, device_id=at_x(d), device_id_type=MESH)
    for there in near:
        pl.semaphore_signal(barrier, inc=1, device_id=there, device_id_type=MESH)

    def tell(level, others):
        for there in others:
            pl.semaphore_signal(heard.at[level], inc=1, device_id=there, device_id_type=MESH)

    lens_in = pltpu.make_async_copy(lens_hbm, lens, lsem.at[0])
    pair_in = pltpu.make_async_copy(pair_hbm, pair, lsem.at[1])
    q_in = pltpu.make_async_copy(q_hbm, qv, lsem.at[2])
    v_in = pltpu.make_async_copy(v_hbm.at[:, pl.ds(pl.multiple_of(x * D, D), D)], vb.at[x], lsem.at[3])
    k_in = [
        pltpu.make_async_copy(k_hbm.at[:, g * D : (g + 1) * D], kb.at[g, 0], lsem.at[4 + g]) for g in range(GROUPS)
    ]
    for one in k_in:
        one.start()
    lens_in.start()
    pair_in.start()
    q_in.start()
    v_in.start()
    for one in k_in:
        one.wait()
    pl.semaphore_wait(barrier, NX - 1 + len(near))

    k_copies = {}
    v_copies = {}
    p_copies = {}
    w_copies = {}
    for i in range(GROUPS):
        for d in (1, 3, 2):
            g = lax.rem(x + d + 1 + i, GROUPS)
            k_copies[d, i] = copy(kb.at[g, 0], kb.at[g, d], k_s.at[d, i], k_r.at[d, i], at_x(d))
            k_copies[d, i].start()
    for d in (1, 3, 2):
        there = lax.rem(x + d, NX)
        v_copies[d] = copy(
            v_hbm.at[:, pl.ds(pl.multiple_of(there * D, D), D)], vb.at[x], v_s.at[d], v_r.at[d], at_x(d)
        )
        v_copies[d].start()
    tell(0, near)
    lens_in.wait()
    pair_in.wait()

    ends = []
    total = 0
    for i in range(DOCS):
        total = total + lens[0, i]
        ends.append(total)

    def segment(places):
        out = jnp.zeros(places.shape, jnp.int32)
        for end in ends:
            out = out + (places >= end).astype(jnp.int32)
        return out

    def iota(shape, axis):
        return lax.broadcasted_iota(jnp.int32, shape, axis)

    q_segment = segment(x * TOK + iota((TOK, TOK), 1))
    row8 = iota((DOCS, D), 0)
    length = jnp.zeros((DOCS, D), F32)
    partner = jnp.zeros((DOCS, D), F32)
    for i in range(DOCS):
        length = jnp.where(row8 == i, lens[0, i].astype(F32), length)
        partner = jnp.where(row8 == i, pair[i].astype(F32), partner)
    prow[mine] = partner
    mst[...] = jnp.zeros_like(mst)
    lst[...] = jnp.ones_like(lst)

    for e in range(NX):
        k_segment = segment(x_from(e) * TOK + iota((TOK, TOK), 0))
        bias[e * TOK : (e + 1) * TOK] = jnp.where(k_segment == q_segment, 0.0, -1e30).astype(F32)

    def scores(part, g):
        places = slice(0, TOK) if part == 0 else slice(TOK, WIN)
        key = kb[g, 0] if part == 0 else kb[g, 1:].reshape(WIN - TOK, D)
        for j in range(PER):
            query = qv[:, pl.ds(pl.multiple_of((g * PER + j) * D, D), D)]
            s = lax.dot_general(key, query, NT, preferred_element_type=F32) * SCALE2 + bias[places]
            m = jnp.max(s, axis=0, keepdims=True)
            p = jnp.exp2(s - m)
            pst[g, places, j * TOK : (j + 1) * TOK] = p.astype(BF16)
            mst[part, g, j : j + 1, :] = m
            lst[part, g, j : j + 1, :] = jnp.sum(p, axis=0, keepdims=True)

    q_in.wait()
    v_in.wait()

    def own(g, carry):
        scores(0, g)
        return carry

    lax.fori_loop(0, GROUPS, own, 0)
    pl.semaphore_wait(heard.at[0], len(near))
    tell(1, [at_z(2), at_z(-2), at_plane(NY // 2 * NC)])

    row16 = lax.rem(iota((2 * DOCS, TOK), 0), DOCS)

    def weigh(g):
        top = jnp.maximum(mst[0, g], mst[1, g])
        fs = [jnp.exp2(mst[part, g] - top) for part in range(2)]
        inv = 1.0 / (lst[0, g] * fs[0] + lst[1, g] * fs[1])
        lhs = []
        for f in fs:
            f = f * inv
            hi = f.astype(BF16).astype(F32)
            both = jnp.concatenate([hi, f - hi], axis=0)
            lhs.append(jnp.concatenate([jnp.where(row16 == j, both, 0.0).astype(BF16) for j in range(PER)], axis=1))
        acc = lax.dot_general(jnp.concatenate(lhs, axis=0), pst[g], NT, preferred_element_type=F32)
        for e in range(NX):
            at = 0 if e == 0 else 2 * DOCS
            half = acc[at : at + 2 * DOCS, e * TOK : (e + 1) * TOK]
            wo[g, :, pl.ds(pl.multiple_of(x_from(e) * TOK, TOK), TOK)] = half[:DOCS] + half[DOCS:]

    def key_copy(d, i):
        g = lax.rem(x + d + 1 + i, GROUPS)
        return copy(kb.at[g, 0], kb.at[g, d], k_s.at[d, i], k_r.at[d, i], at_x(d))

    def step(i, carry):
        group = lax.rem(x + 1 + i, GROUPS)

        for d in (1, 3, 2):
            key_copy(d, i).wait_recv()
        scores(1, group)
        weigh(group)

        @pl.when(i < GROUPS - 1)
        def _():
            copy(wo.at[group], wi.at[x], w_s.at[i + 1], w_r.at[i + 1], at_x(i + 1)).start()

        @pl.when(i == 0)
        def _():
            pl.semaphore_wait(heard.at[1], 3)
            tell(2, [at_z(4), at_z(-4)])

        return carry

    lax.fori_loop(0, GROUPS, step, 0)
    pl.semaphore_wait(heard.at[2], 2)
    for d in range(1, NX):
        group = lax.rem(x + d, GROUPS)
        w_copies[d] = copy(wo.at[group], wi.at[x], w_s.at[d], w_r.at[d], at_x(d))
    for k in range(1, PLANE):
        p_copies[k] = copy(prow.at[mine], prow.at[mine], p_s.at[k], p_r.at[k], at_plane(k))
        p_copies[k].start()
    onehot = (segment(iota((DOCS, WIN), 1)) == iota((DOCS, WIN), 0)).astype(F32)
    for d in (1, 3, 2):
        v_copies[d].wait_recv()
    weights = wo[x]
    for d in (1, 3, 2):
        w_copies[d].wait_recv()
        weights = weights + wi[x_from(d)]
    lhs = jnp.concatenate([weights[j : j + 1] * onehot for j in range(PER)], axis=0)
    hi, lo = split2(lhs)
    sums = jnp.dot(jnp.concatenate([hi, lo], axis=0), vb[...].reshape(WIN, D), preferred_element_type=F32)
    sums = sums[: PER * DOCS] + sums[PER * DOCS :]
    per_length = 1.0 / length
    for j in range(PER):
        pooled[:, j * D : (j + 1) * D] = sums[j * DOCS : (j + 1) * DOCS] * per_length
    short = pooled[...].astype(BF16)
    ucol[z] = short
    urow[mine] = short

    c_copies = {}
    u_copies = {}

    def send_col(origin, step, offset):
        c_copies[offset] = copy(ucol.at[origin], ucol.at[origin], c_s.at[offset % NZ], c_r.at[offset % NZ], at_z(step))
        c_copies[offset].start()

    for o in FAR + (8,) + NEAR:
        send_col(z, o, o)
    for k in range(1, PLANE):
        u_copies[k] = copy(urow.at[mine], urow.at[mine], u_s.at[k], u_r.at[k], at_plane(k))
        u_copies[k].start()
    for o in FAR:
        c_copies[o].wait_recv()
        for step in FORWARD[o]:
            send_col(z_from(o), step, o + step)
    for k in range(1, PLANE):
        u_copies[k].wait_recv()

    def squares(a):
        wide = a.astype(F32)
        return jnp.sum(wide * wide, axis=1, keepdims=True)

    def to_row(column):
        n = column.shape[0]
        return jnp.sum(jnp.where(iota((n, D), 0) == iota((n, D), 1), column, 0.0), axis=0, keepdims=True)

    rows = urow[...].reshape(ROWS, FEAT)
    dsend[ROWS:, :] = jnp.broadcast_to(to_row(squares(rows)), (DOCS, D))
    for o in c_copies:
        if o not in FAR:
            c_copies[o].wait_recv()
    cols = ucol[...].reshape(COLS, FEAT)
    dsend[:ROWS, :] = lax.dot_general(rows, cols, NT, preferred_element_type=F32)
    dsend[ROWS : ROWS + 1, :] = to_row(squares(cols))
    d_copies = {d: copy(dsend, drecv.at[x], d_s.at[d], d_r.at[d], at_x(d)) for d in (2, 1, 3)}
    for d in d_copies:
        d_copies[d].start()
    for d in (1, 3, 2):
        d_copies[d].wait_recv()
    full = dsend[...]
    for d in range(1, NX):
        full = full + drecv[x_from(d)]

    r_id, c_id = iota((ROWS, COLS), 0), iota((ROWS, COLS), 1)
    eye = r_id == c_id

    def to_column(row):
        return jnp.sum(jnp.where(eye, row, 0.0), axis=1, keepdims=True)

    inv_rows = 1.0 / jnp.sqrt(to_column(full[ROWS + 1 : ROWS + 2]) + 1e-6)
    inv_cols = INV_TEMP / jnp.sqrt(full[ROWS : ROWS + 1] + 1e-6)
    logits = full[:ROWS] * (inv_rows * inv_cols)
    r_plane, r_doc = r_id // DOCS, lax.rem(r_id, DOCS)
    c_z, c_doc = c_id // DOCS, lax.rem(c_id, DOCS)
    same = (r_plane == mine) & (c_z == z) & (r_doc == c_doc)
    weight = jnp.where(same, 0.0, jnp.exp(logits))
    col_sum = jnp.sum(weight, axis=0, keepdims=True)
    ssend[...] = jnp.broadcast_to(col_sum, (DOCS, D))
    t_copies = {}
    a_copies = {}
    for o in (8, 7, -7, 6, -6, 5, -5, 4, -4, 3, -3, 2, -2, 1, -1):
        t_copies[o] = copy(ssend.at[pl.ds(0, 1)], scol.at[z, pl.ds(0, 1)], t_s.at[o % NZ], t_r.at[o % NZ], at_z(o))
        t_copies[o].start()
    row_sum = to_row(jnp.sum(weight, axis=1, keepdims=True))
    rsend[...] = jnp.broadcast_to(row_sum, (DOCS, D))
    for k in range(1, PLANE):
        a_copies[k] = copy(rsend.at[pl.ds(0, 1)], srow.at[mine, pl.ds(0, 1)], a_s.at[k], a_r.at[k], at_plane(k))
        a_copies[k].start()

    norms[...] = jnp.broadcast_to(inv_rows, (ROWS, D))
    own_inverse = norms[pl.ds(pl.multiple_of(mine * DOCS, DOCS), DOCS), :]
    for j in range(PER):
        at = slice(j * D, (j + 1) * D)
        out[:, at] = pooled[:, at] * own_inverse
    for k in p_copies:
        p_copies[k].wait_recv()
    partners = prow[...].reshape(ROWS, D)
    column_doc = ((y * NZ + c_z) * NC + c) * DOCS + c_doc
    pairs = jnp.where(partners == column_doc.astype(F32), 2.0, 0.0)
    for k in range(1, PLANE):
        a_copies[k].wait_recv()
        row_sum = row_sum + srow[slot_from(k), 0:1, :]
    scale = inv_rows * inv_cols
    ready = (weight * (1.0 / to_column(row_sum)) - pairs) * scale
    scaled_weight = weight * scale
    undone = full[:ROWS] * inv_rows
    for o in reversed(list(t_copies)):
        t_copies[o].wait_recv()
        col_sum = col_sum + scol[z_from(o), 0:1, :]
    scaled = scaled_weight * (1.0 / col_sum) + ready
    along = jnp.sum(scaled * undone, axis=1, keepdims=True)
    hi, lo = split2(scaled)
    parts = jnp.dot(jnp.concatenate([hi, lo], axis=0), cols, preferred_element_type=F32)
    gsend[:, :, :FEAT] = (parts[:ROWS] + parts[ROWS:]).astype(BF16).reshape(PLANE, DOCS, FEAT)
    gsend[:, :, FEAT:] = jnp.broadcast_to(along, (ROWS, D)).astype(BF16).reshape(PLANE, DOCS, D)
    g_copies = {}
    for k in (5, 4, 7, 3, 6, 2, 1):
        g_copies[k] = copy(gsend.at[slot_to(k)], grecv.at[mine], g_s.at[k], g_r.at[k], at_plane(k))
        g_copies[k].start()
    gradient = gsend[mine].astype(F32)
    for k in range(1, PLANE):
        g_copies[k].wait_recv()
        gradient = gradient + grecv[slot_from(k)].astype(F32)
    out[:, FEAT:] = gradient

    for copies in (
        k_copies, v_copies, p_copies, w_copies, c_copies, u_copies, d_copies, t_copies, a_copies, g_copies
    ):
        for key in copies:
            copies[key].wait_send()


def per_device(queries, keys, values, document_lengths, pair_ids):
    dma = pltpu.SemaphoreType.DMA
    vmem = pl.BlockSpec(memory_space=pltpu.VMEM)
    hbm = pl.BlockSpec(memory_space=pl.ANY)
    both = pl.pallas_call(
        kernel,
        out_shape=jax.ShapeDtypeStruct((DOCS, 2 * FEAT + D), F32),
        in_specs=[hbm] * 5,
        out_specs=vmem,
        scratch_shapes=[
            pltpu.SMEM((1, DOCS), jnp.int32),
            pltpu.SMEM((DOCS,), jnp.int32),
            pltpu.VMEM((TOK, HEADS * D), BF16),
            pltpu.VMEM((GROUPS, NX, TOK, D), BF16),
            pltpu.VMEM((NX, TOK, D), BF16),
            pltpu.VMEM((WIN, TOK), F32),
            pltpu.VMEM((GROUPS, WIN, PER * TOK), BF16),
            pltpu.VMEM((2, GROUPS, DOCS, TOK), F32),
            pltpu.VMEM((2, GROUPS, DOCS, TOK), F32),
            pltpu.VMEM((GROUPS, DOCS, WIN), F32),
            pltpu.VMEM((NX, DOCS, WIN), F32),
            pltpu.VMEM((DOCS, FEAT), F32),
            pltpu.VMEM((NZ, DOCS, FEAT), BF16),
            pltpu.VMEM((PLANE, DOCS, FEAT), BF16),
            pltpu.VMEM((PLANE, DOCS, D), F32),
            pltpu.VMEM((ROWS + DOCS, COLS), F32),
            pltpu.VMEM((NX, ROWS + DOCS, COLS), F32),
            pltpu.VMEM((DOCS, D), F32),
            pltpu.VMEM((NZ, DOCS, D), F32),
            pltpu.VMEM((DOCS, D), F32),
            pltpu.VMEM((PLANE, DOCS, D), F32),
            pltpu.VMEM((PLANE, DOCS, FEAT + D), BF16),
            pltpu.VMEM((PLANE, DOCS, FEAT + D), BF16),
            pltpu.VMEM((ROWS, D), F32),
            pltpu.SemaphoreType.REGULAR((3,)),
            dma((4 + GROUPS,)),
            dma((NX, GROUPS)), dma((NX, GROUPS)),
            dma((NX,)), dma((NX,)),
            dma((NX,)), dma((NX,)),
            dma((PLANE,)), dma((PLANE,)),
            dma((PLANE,)), dma((PLANE,)),
            dma((NZ,)), dma((NZ,)),
            dma((NX,)), dma((NX,)),
            dma((NZ,)), dma((NZ,)),
            dma((PLANE,)), dma((PLANE,)),
            dma((PLANE,)), dma((PLANE,)),
        ],
        compiler_params=pltpu.CompilerParams(
            collective_id=0, has_side_effects=True, vmem_limit_bytes=60 << 20
        ),
    )(document_lengths, pair_ids, queries, keys, values)
    embeddings = both[:, :FEAT].astype(BF16)
    grads = both[:, FEAT : 2 * FEAT] - embeddings.astype(F32) * both[:, 2 * FEAT : 2 * FEAT + 1]
    return embeddings, grads


def solution(mesh):
    return jax.shard_map(
        per_device,
        mesh=mesh,
        in_specs=(
            P(("dp", "sp"), None),
            P(("dp", "sp"), None),
            P(("dp", "sp"), None),
            P("dp", None),
            P("dp"),
        ),
        out_specs=(P("dp", "sp"), P("dp", "sp")),
        check_vma=False,
    )
```

```python
import functools
import math

import jax
import jax.numpy as jnp
from jax import lax
from jax.experimental import pallas as pl
from jax.experimental.pallas import tpu as pltpu
from jax.sharding import PartitionSpec as P

MESH = pl.DeviceIdType.MESH
F32 = jnp.float32
BF16 = jnp.bfloat16
NT = (((1,), (1,)), ((), ()))

GROUPS = 4
PER = 7
HEADS = GROUPS * PER
D = 128
DOCS = 8
TOK = 128
WIN = 512
FEAT = PER * D
NX, NY, NZ, NC = 4, 4, 16, 2
PLANE = NY * NC
ROWS = PLANE * DOCS
COLS = NZ * DOCS
INV_TEMP = 50.0
SCALE2 = D ** (-0.5) * math.log2(math.e)

NEAR = ()
FAR = (1, -1, 5, -5)
FORWARD = {1: (1,), -1: (-1,), 5: (1, -2, -1), -5: (-1, 2, 1)}


def split2(a):
    hi = a.astype(BF16)
    return hi, (a - hi.astype(F32)).astype(BF16)


def kernel(
    lens_hbm, pair_hbm, q_hbm, k_hbm, v_hbm, out_hbm,
    lens, pair, qv, kb, vb, bias, pst, mst, lst, wo, wi, pooled, ucol, urow, prow,
    dsend, drecv, ssend, scol, rsend, srow, gsend, grecv, norms, out,
    heard, osem, lsem, k_s, k_r, v_s, v_r, w_s, w_r, p_s, p_r, u_s, u_r, c_s, c_r, d_s, d_r, t_s, t_r, a_s, a_r, g_s, g_r,
):
    dp = lax.axis_index("dp")
    x = lax.axis_index("sp")
    c = lax.rem(dp, NC)
    z = lax.rem(dp // NC, NZ)
    y = dp // (NC * NZ)
    mine = y * NC + c

    def at_x(d):
        return (dp, lax.rem(x + d, NX))

    def at_z(o):
        return ((y * NZ + lax.rem(z + o + NZ, NZ)) * NC + c, x)

    def at_plane(k):
        there_y, there_c = lax.rem(y + k // NC, NY), lax.rem(c + k % NC, NC)
        return ((there_y * NZ + z) * NC + there_c, x)

    def slot_to(k):
        return lax.rem(y + k // NC, NY) * NC + lax.rem(c + k % NC, NC)

    def slot_from(k):
        return lax.rem(y - k // NC + NY, NY) * NC + lax.rem(c + k % NC, NC)

    def z_from(o):
        return lax.rem(z - o + NZ, NZ)

    def x_from(d):
        return lax.rem(x - d + NX, NX)

    def copy(src, dst, ss, rs, there):
        return pltpu.make_async_remote_copy(
            src_ref=src, dst_ref=dst, send_sem=ss, recv_sem=rs, device_id=there, device_id_type=MESH
        )

    near = [at_plane(1), at_plane(NC), at_plane((NY - 1) * NC), at_z(1), at_z(-1)]
    barrier = pltpu.get_barrier_semaphore()
    for d in (2, 1, 3):
        pl.semaphore_signal(barrier, inc=1, device_id=at_x(d), device_id_type=MESH)
    for there in near:
        pl.semaphore_signal(barrier, inc=1, device_id=there, device_id_type=MESH)

    def tell(level, others):
        for there in others:
            pl.semaphore_signal(heard.at[level], inc=1, device_id=there, device_id_type=MESH)

    lens_in = pltpu.make_async_copy(lens_hbm, lens, lsem.at[0])
    pair_in = pltpu.make_async_copy(pair_hbm, pair, lsem.at[1])
    q_in = pltpu.make_async_copy(q_hbm, qv, lsem.at[2])
    v_in = pltpu.make_async_copy(v_hbm.at[:, pl.ds(pl.multiple_of(x * D, D), D)], vb.at[x], lsem.at[3])
    k_in = [
        pltpu.make_async_copy(k_hbm.at[:, g * D : (g + 1) * D], kb.at[g, 0], lsem.at[4 + g]) for g in range(GROUPS)
    ]
    for one in k_in:
        one.start()
    lens_in.start()
    pair_in.start()
    q_in.start()
    v_in.start()
    for one in k_in:
        one.wait()
    pl.semaphore_wait(barrier, NX - 1 + len(near))

    k_copies = {}
    v_copies = {}
    p_copies = {}
    w_copies = {}
    for i in range(GROUPS):
        for d in (1, 3, 2):
            g = lax.rem(x + d + 1 + i, GROUPS)
            k_copies[d, i] = copy(kb.at[g, 0], kb.at[g, d], k_s.at[d, i], k_r.at[d, i], at_x(d))
            k_copies[d, i].start()
    for d in (1, 3, 2):
        there = lax.rem(x + d, NX)
        v_copies[d] = copy(
            v_hbm.at[:, pl.ds(pl.multiple_of(there * D, D), D)], vb.at[x], v_s.at[d], v_r.at[d], at_x(d)
        )
        v_copies[d].start()
    tell(0, near)
    lens_in.wait()
    pair_in.wait()

    ends = []
    total = 0
    for i in range(DOCS):
        total = total + lens[0, i]
        ends.append(total)

    def segment(places):
        out = jnp.zeros(places.shape, jnp.int32)
        for end in ends:
            out = out + (places >= end).astype(jnp.int32)
        return out

    def iota(shape, axis):
        return lax.broadcasted_iota(jnp.int32, shape, axis)

    q_segment = segment(x * TOK + iota((TOK, TOK), 1))
    row8 = iota((DOCS, D), 0)
    length = jnp.zeros((DOCS, D), F32)
    partner = jnp.zeros((DOCS, D), F32)
    for i in range(DOCS):
        length = jnp.where(row8 == i, lens[0, i].astype(F32), length)
        partner = jnp.where(row8 == i, pair[i].astype(F32), partner)
    prow[mine] = partner
    mst[...] = jnp.zeros_like(mst)
    lst[...] = jnp.ones_like(lst)

    for e in range(NX):
        k_segment = segment(x_from(e) * TOK + iota((TOK, TOK), 0))
        bias[e * TOK : (e + 1) * TOK] = jnp.where(k_segment == q_segment, 0.0, -1e30).astype(F32)

    def scores(part, g):
        places = slice(0, TOK) if part == 0 else slice(TOK, WIN)
        key = kb[g, 0] if part == 0 else kb[g, 1:].reshape(WIN - TOK, D)
        for j in range(PER):
            query = qv[:, pl.ds(pl.multiple_of((g * PER + j) * D, D), D)]
            s = lax.dot_general(key, query, NT, preferred_element_type=F32) * SCALE2 + bias[places]
            m = jnp.max(s, axis=0, keepdims=True)
            p = jnp.exp2(s - m)
            pst[g, places, j * TOK : (j + 1) * TOK] = p.astype(BF16)
            mst[part, g, j : j + 1, :] = m
            lst[part, g, j : j + 1, :] = jnp.sum(p, axis=0, keepdims=True)

    q_in.wait()
    v_in.wait()

    def own(g, carry):
        scores(0, g)
        return carry

    lax.fori_loop(0, GROUPS, own, 0)
    pl.semaphore_wait(heard.at[0], len(near))
    tell(1, [at_z(2), at_z(-2), at_plane(NY // 2 * NC)])

    row16 = lax.rem(iota((2 * DOCS, TOK), 0), DOCS)

    def weigh(g):
        top = jnp.maximum(mst[0, g], mst[1, g])
        fs = [jnp.exp2(mst[part, g] - top) for part in range(2)]
        inv = 1.0 / (lst[0, g] * fs[0] + lst[1, g] * fs[1])
        lhs = []
        for f in fs:
            f = f * inv
            hi = f.astype(BF16).astype(F32)
            both = jnp.concatenate([hi, f - hi], axis=0)
            lhs.append(jnp.concatenate([jnp.where(row16 == j, both, 0.0).astype(BF16) for j in range(PER)], axis=1))
        acc = lax.dot_general(jnp.concatenate(lhs, axis=0), pst[g], NT, preferred_element_type=F32)
        for e in range(NX):
            at = 0 if e == 0 else 2 * DOCS
            half = acc[at : at + 2 * DOCS, e * TOK : (e + 1) * TOK]
            wo[g, :, pl.ds(pl.multiple_of(x_from(e) * TOK, TOK), TOK)] = half[:DOCS] + half[DOCS:]

    def key_copy(d, i):
        g = lax.rem(x + d + 1 + i, GROUPS)
        return copy(kb.at[g, 0], kb.at[g, d], k_s.at[d, i], k_r.at[d, i], at_x(d))

    def step(i, carry):
        group = lax.rem(x + 1 + i, GROUPS)

        for d in (1, 3, 2):
            key_copy(d, i).wait_recv()
        scores(1, group)
        weigh(group)

        @pl.when(i < GROUPS - 1)
        def _():
            copy(wo.at[group], wi.at[x], w_s.at[i + 1], w_r.at[i + 1], at_x(i + 1)).start()

        @pl.when(i == 0)
        def _():
            pl.semaphore_wait(heard.at[1], 3)
            tell(2, [at_z(4), at_z(-4)])

        return carry

    lax.fori_loop(0, GROUPS, step, 0)
    pl.semaphore_wait(heard.at[2], 2)
    for d in range(1, NX):
        group = lax.rem(x + d, GROUPS)
        w_copies[d] = copy(wo.at[group], wi.at[x], w_s.at[d], w_r.at[d], at_x(d))
    for k in range(1, PLANE):
        p_copies[k] = copy(prow.at[mine], prow.at[mine], p_s.at[k], p_r.at[k], at_plane(k))
        p_copies[k].start()
    onehot = (segment(iota((DOCS, WIN), 1)) == iota((DOCS, WIN), 0)).astype(F32)
    for d in (1, 3, 2):
        v_copies[d].wait_recv()
    weights = wo[x]
    for d in (1, 3, 2):
        w_copies[d].wait_recv()
        weights = weights + wi[x_from(d)]
    lhs = jnp.concatenate([weights[j : j + 1] * onehot for j in range(PER)], axis=0)
    hi, lo = split2(lhs)
    sums = jnp.dot(jnp.concatenate([hi, lo], axis=0), vb[...].reshape(WIN, D), preferred_element_type=F32)
    sums = sums[: PER * DOCS] + sums[PER * DOCS :]
    per_length = 1.0 / length
    for j in range(PER):
        pooled[:, j * D : (j + 1) * D] = sums[j * DOCS : (j + 1) * DOCS] * per_length
    short = pooled[...].astype(BF16)
    ucol[z] = short
    urow[mine] = short

    c_copies = {}
    u_copies = {}

    def send_col(origin, step, offset):
        c_copies[offset] = copy(ucol.at[origin], ucol.at[origin], c_s.at[offset % NZ], c_r.at[offset % NZ], at_z(step))
        c_copies[offset].start()

    for o in (5, -5, 7, -7, 8, 1, -1):
        send_col(z, o, o)
    for k in range(1, PLANE):
        u_copies[k] = copy(urow.at[mine], urow.at[mine], u_s.at[k], u_r.at[k], at_plane(k))
        u_copies[k].start()
    for o in FAR:
        c_copies[o].wait_recv()
        for step in FORWARD[o]:
            send_col(z_from(o), step, o + step)
    for k in range(1, PLANE):
        u_copies[k].wait_recv()

    def squares(a):
        wide = a.astype(F32)
        return jnp.sum(wide * wide, axis=1, keepdims=True)

    def to_row(column):
        n = column.shape[0]
        return jnp.sum(jnp.where(iota((n, D), 0) == iota((n, D), 1), column, 0.0), axis=0, keepdims=True)

    rows = urow[...].reshape(ROWS, FEAT)
    dsend[ROWS:, :] = jnp.broadcast_to(to_row(squares(rows)), (DOCS, D))
    for o in c_copies:
        if o not in FAR:
            c_copies[o].wait_recv()
    cols = ucol[...].reshape(COLS, FEAT)
    dsend[:ROWS, :] = lax.dot_general(rows, cols, NT, preferred_element_type=F32)
    dsend[ROWS : ROWS + 1, :] = to_row(squares(cols))
    d_copies = {d: copy(dsend, drecv.at[x], d_s.at[d], d_r.at[d], at_x(d)) for d in (2, 1, 3)}
    for d in d_copies:
        d_copies[d].start()
    for d in (1, 3, 2):
        d_copies[d].wait_recv()
    full = dsend[...]
    for d in range(1, NX):
        full = full + drecv[x_from(d)]

    r_id, c_id = iota((ROWS, COLS), 0), iota((ROWS, COLS), 1)
    eye = r_id == c_id

    def to_column(row):
        return jnp.sum(jnp.where(eye, row, 0.0), axis=1, keepdims=True)

    inv_rows = 1.0 / jnp.sqrt(to_column(full[ROWS + 1 : ROWS + 2]) + 1e-6)
    inv_cols = INV_TEMP / jnp.sqrt(full[ROWS : ROWS + 1] + 1e-6)
    logits = full[:ROWS] * (inv_rows * inv_cols)
    r_plane, r_doc = r_id // DOCS, lax.rem(r_id, DOCS)
    c_z, c_doc = c_id // DOCS, lax.rem(c_id, DOCS)
    same = (r_plane == mine) & (c_z == z) & (r_doc == c_doc)
    weight = jnp.where(same, 0.0, jnp.exp(logits))
    col_sum = jnp.sum(weight, axis=0, keepdims=True)
    ssend[...] = jnp.broadcast_to(col_sum, (DOCS, D))
    t_copies = {}
    a_copies = {}
    for o in (8, 7, -7, 6, -6, 5, -5, 4, -4, 3, -3, 2, -2, 1, -1):
        t_copies[o] = copy(ssend.at[pl.ds(0, 1)], scol.at[z, pl.ds(0, 1)], t_s.at[o % NZ], t_r.at[o % NZ], at_z(o))
        t_copies[o].start()
    row_sum = to_row(jnp.sum(weight, axis=1, keepdims=True))
    rsend[...] = jnp.broadcast_to(row_sum, (DOCS, D))
    for k in range(1, PLANE):
        a_copies[k] = copy(rsend.at[pl.ds(0, 1)], srow.at[mine, pl.ds(0, 1)], a_s.at[k], a_r.at[k], at_plane(k))
        a_copies[k].start()

    norms[...] = jnp.broadcast_to(inv_rows, (ROWS, D))
    own_inverse = norms[pl.ds(pl.multiple_of(mine * DOCS, DOCS), DOCS), :]
    for j in range(PER):
        at = slice(j * D, (j + 1) * D)
        out[:, at] = pooled[:, at] * own_inverse
    emb_out = pltpu.make_async_copy(out.at[:, pl.ds(0, FEAT)], out_hbm.at[:, pl.ds(0, FEAT)], osem.at[0])
    emb_out.start()
    for k in p_copies:
        p_copies[k].wait_recv()
    partners = prow[...].reshape(ROWS, D)
    column_doc = ((y * NZ + c_z) * NC + c) * DOCS + c_doc
    pairs = jnp.where(partners == column_doc.astype(F32), 2.0, 0.0)
    for k in range(1, PLANE):
        a_copies[k].wait_recv()
        row_sum = row_sum + srow[slot_from(k), 0:1, :]
    scale = inv_rows * inv_cols
    ready = (weight * (1.0 / to_column(row_sum)) - pairs) * scale
    scaled_weight = weight * scale
    undone = full[:ROWS] * inv_rows
    for o in reversed(list(t_copies)):
        t_copies[o].wait_recv()
        col_sum = col_sum + scol[z_from(o), 0:1, :]
    scaled = scaled_weight * (1.0 / col_sum) + ready
    along = jnp.sum(scaled * undone, axis=1, keepdims=True)
    hi, lo = split2(scaled)
    parts = jnp.dot(jnp.concatenate([hi, lo], axis=0), cols, preferred_element_type=F32)
    gsend[:, :, :FEAT] = (parts[:ROWS] + parts[ROWS:]).astype(BF16).reshape(PLANE, DOCS, FEAT)
    gsend[:, :, FEAT:] = jnp.broadcast_to(along, (ROWS, D)).astype(BF16).reshape(PLANE, DOCS, D)
    g_copies = {}
    for k in (5, 4, 7, 3, 6, 2, 1):
        g_copies[k] = copy(gsend.at[slot_to(k)], grecv.at[mine], g_s.at[k], g_r.at[k], at_plane(k))
        g_copies[k].start()
    gradient = gsend[mine].astype(F32)
    for k in range(1, PLANE):
        g_copies[k].wait_recv()
        gradient = gradient + grecv[slot_from(k)].astype(F32)
    out[:, FEAT:] = gradient
    grad_out = pltpu.make_async_copy(out.at[:, pl.ds(FEAT, FEAT + D)], out_hbm.at[:, pl.ds(FEAT, FEAT + D)], osem.at[1])
    grad_out.start()

    for copies in (
        k_copies, v_copies, p_copies, w_copies, c_copies, u_copies, d_copies, t_copies, a_copies, g_copies
    ):
        for key in copies:
            copies[key].wait_send()
    emb_out.wait()
    grad_out.wait()


def per_device(queries, keys, values, document_lengths, pair_ids):
    dma = pltpu.SemaphoreType.DMA
    hbm = pl.BlockSpec(memory_space=pl.ANY)
    both = pl.pallas_call(
        kernel,
        out_shape=jax.ShapeDtypeStruct((DOCS, 2 * FEAT + D), F32),
        in_specs=[hbm] * 5,
        out_specs=hbm,
        scratch_shapes=[
            pltpu.SMEM((1, DOCS), jnp.int32),
            pltpu.SMEM((DOCS,), jnp.int32),
            pltpu.VMEM((TOK, HEADS * D), BF16),
            pltpu.VMEM((GROUPS, NX, TOK, D), BF16),
            pltpu.VMEM((NX, TOK, D), BF16),
            pltpu.VMEM((WIN, TOK), F32),
            pltpu.VMEM((GROUPS, WIN, PER * TOK), BF16),
            pltpu.VMEM((2, GROUPS, DOCS, TOK), F32),
            pltpu.VMEM((2, GROUPS, DOCS, TOK), F32),
            pltpu.VMEM((GROUPS, DOCS, WIN), F32),
            pltpu.VMEM((NX, DOCS, WIN), F32),
            pltpu.VMEM((DOCS, FEAT), F32),
            pltpu.VMEM((NZ, DOCS, FEAT), BF16),
            pltpu.VMEM((PLANE, DOCS, FEAT), BF16),
            pltpu.VMEM((PLANE, DOCS, D), F32),
            pltpu.VMEM((ROWS + DOCS, COLS), F32),
            pltpu.VMEM((NX, ROWS + DOCS, COLS), F32),
            pltpu.VMEM((DOCS, D), F32),
            pltpu.VMEM((NZ, DOCS, D), F32),
            pltpu.VMEM((DOCS, D), F32),
            pltpu.VMEM((PLANE, DOCS, D), F32),
            pltpu.VMEM((PLANE, DOCS, FEAT + D), BF16),
            pltpu.VMEM((PLANE, DOCS, FEAT + D), BF16),
            pltpu.VMEM((ROWS, D), F32),
            pltpu.VMEM((DOCS, 2 * FEAT + D), F32),
            pltpu.SemaphoreType.REGULAR((3,)),
            dma((2,)),
            dma((4 + GROUPS,)),
            dma((NX, GROUPS)), dma((NX, GROUPS)),
            dma((NX,)), dma((NX,)),
            dma((NX,)), dma((NX,)),
            dma((PLANE,)), dma((PLANE,)),
            dma((PLANE,)), dma((PLANE,)),
            dma((NZ,)), dma((NZ,)),
            dma((NX,)), dma((NX,)),
            dma((NZ,)), dma((NZ,)),
            dma((PLANE,)), dma((PLANE,)),
            dma((PLANE,)), dma((PLANE,)),
        ],
        compiler_params=pltpu.CompilerParams(
            collective_id=0, has_side_effects=True, vmem_limit_bytes=60 << 20
        ),
    )(document_lengths, pair_ids, queries, keys, values)
    embeddings = both[:, :FEAT].astype(BF16)
    grads = both[:, FEAT : 2 * FEAT] - embeddings.astype(F32) * both[:, 2 * FEAT : 2 * FEAT + 1]
    return embeddings, grads


def solution(mesh):
    return jax.shard_map(
        per_device,
        mesh=mesh,
        in_specs=(
            P(("dp", "sp"), None),
            P(("dp", "sp"), None),
            P(("dp", "sp"), None),
            P("dp", None),
            P("dp"),
        ),
        out_specs=(P("dp", "sp"), P("dp", "sp")),
        check_vma=False,
    )
```

```python
import functools
import math

import jax
import jax.numpy as jnp
from jax import lax
from jax.experimental import pallas as pl
from jax.experimental.pallas import tpu as pltpu
from jax.sharding import PartitionSpec as P

MESH = pl.DeviceIdType.MESH
F32 = jnp.float32
BF16 = jnp.bfloat16
NT = (((1,), (1,)), ((), ()))

GROUPS = 4
PER = 7
HEADS = GROUPS * PER
D = 128
DOCS = 8
TOK = 128
WIN = 512
FEAT = PER * D
NX, NY, NZ, NC = 4, 4, 16, 2
PLANE = NY * NC
ROWS = PLANE * DOCS
COLS = NZ * DOCS
INV_TEMP = 50.0
SCALE2 = D ** (-0.5) * math.log2(math.e)

NEAR = ()
FAR = (1, -1, 5, -5)
FORWARD = {1: (1,), -1: (-1,), 5: (1, -2, -1), -5: (-1, 2, 1)}


def split2(a):
    hi = a.astype(BF16)
    return hi, (a - hi.astype(F32)).astype(BF16)


def kernel(
    lens_hbm, pair_hbm, q_hbm, k_hbm, v_hbm, out_hbm,
    lens, pair, qv, kb, vb, bias, pst, mst, lst, wo, wi, pooled, ucol, urow, prow,
    dsend, drecv, ssend, scol, rsend, srow, gsend, grecv, norms, out,
    heard, osem, lsem, k_s, k_r, v_s, v_r, w_s, w_r, p_s, p_r, u_s, u_r, c_s, c_r, d_s, d_r, t_s, t_r, a_s, a_r, g_s, g_r,
):
    dp = lax.axis_index("dp")
    x = lax.axis_index("sp")
    c = lax.rem(dp, NC)
    z = lax.rem(dp // NC, NZ)
    y = dp // (NC * NZ)
    mine = y * NC + c

    def at_x(d):
        return (dp, lax.rem(x + d, NX))

    def at_z(o):
        return ((y * NZ + lax.rem(z + o + NZ, NZ)) * NC + c, x)

    def at_plane(k):
        there_y, there_c = lax.rem(y + k // NC, NY), lax.rem(c + k % NC, NC)
        return ((there_y * NZ + z) * NC + there_c, x)

    def slot_to(k):
        return lax.rem(y + k // NC, NY) * NC + lax.rem(c + k % NC, NC)

    def slot_from(k):
        return lax.rem(y - k // NC + NY, NY) * NC + lax.rem(c + k % NC, NC)

    def z_from(o):
        return lax.rem(z - o + NZ, NZ)

    def x_from(d):
        return lax.rem(x - d + NX, NX)

    def copy(src, dst, ss, rs, there):
        return pltpu.make_async_remote_copy(
            src_ref=src, dst_ref=dst, send_sem=ss, recv_sem=rs, device_id=there, device_id_type=MESH
        )

    near = [at_plane(1), at_plane(NC), at_plane((NY - 1) * NC), at_z(1), at_z(-1)]
    barrier = pltpu.get_barrier_semaphore()
    for d in (2, 1, 3):
        pl.semaphore_signal(barrier, inc=1, device_id=at_x(d), device_id_type=MESH)
    for there in near:
        pl.semaphore_signal(barrier, inc=1, device_id=there, device_id_type=MESH)

    def tell(level, others):
        for there in others:
            pl.semaphore_signal(heard.at[level], inc=1, device_id=there, device_id_type=MESH)

    lens_in = pltpu.make_async_copy(lens_hbm, lens, lsem.at[0])
    pair_in = pltpu.make_async_copy(pair_hbm, pair, lsem.at[1])
    q_in = pltpu.make_async_copy(q_hbm, qv, lsem.at[2])
    v_in = pltpu.make_async_copy(v_hbm.at[:, pl.ds(pl.multiple_of(x * D, D), D)], vb.at[x], lsem.at[3])
    k_in = [
        pltpu.make_async_copy(k_hbm.at[:, g * D : (g + 1) * D], kb.at[g, 0], lsem.at[4 + g]) for g in range(GROUPS)
    ]
    for one in k_in:
        one.start()
    lens_in.start()
    pair_in.start()
    q_in.start()
    v_in.start()
    for one in k_in:
        one.wait()
    pl.semaphore_wait(barrier, NX - 1 + len(near))

    k_copies = {}
    v_copies = {}
    p_copies = {}
    w_copies = {}
    for i in range(GROUPS):
        for d in (1, 3, 2):
            g = lax.rem(x + d + 1 + i, GROUPS)
            k_copies[d, i] = copy(kb.at[g, 0], kb.at[g, d], k_s.at[d, i], k_r.at[d, i], at_x(d))
            k_copies[d, i].start()
    for d in (1, 3, 2):
        there = lax.rem(x + d, NX)
        v_copies[d] = copy(
            v_hbm.at[:, pl.ds(pl.multiple_of(there * D, D), D)], vb.at[x], v_s.at[d], v_r.at[d], at_x(d)
        )
        v_copies[d].start()
    tell(0, near)
    lens_in.wait()
    pair_in.wait()

    ends = []
    total = 0
    for i in range(DOCS):
        total = total + lens[0, i]
        ends.append(total)

    def segment(places):
        out = jnp.zeros(places.shape, jnp.int32)
        for end in ends:
            out = out + (places >= end).astype(jnp.int32)
        return out

    def iota(shape, axis):
        return lax.broadcasted_iota(jnp.int32, shape, axis)

    q_segment = segment(x * TOK + iota((TOK, TOK), 1))
    row8 = iota((DOCS, D), 0)
    length = jnp.zeros((DOCS, D), F32)
    partner = jnp.zeros((DOCS, D), F32)
    for i in range(DOCS):
        length = jnp.where(row8 == i, lens[0, i].astype(F32), length)
        partner = jnp.where(row8 == i, pair[i].astype(F32), partner)
    prow[mine] = partner
    mst[...] = jnp.zeros_like(mst)
    lst[...] = jnp.ones_like(lst)

    for e in range(NX):
        k_segment = segment(x_from(e) * TOK + iota((TOK, TOK), 0))
        bias[e * TOK : (e + 1) * TOK] = jnp.where(k_segment == q_segment, 0.0, -1e30).astype(F32)

    def scores(part, g):
        places = slice(0, TOK) if part == 0 else slice(TOK, WIN)
        key = kb[g, 0] if part == 0 else kb[g, 1:].reshape(WIN - TOK, D)
        for j in range(PER):
            query = qv[:, pl.ds(pl.multiple_of((g * PER + j) * D, D), D)]
            s = lax.dot_general(key, query, NT, preferred_element_type=F32) * SCALE2 + bias[places]
            m = jnp.max(s, axis=0, keepdims=True)
            p = jnp.exp2(s - m)
            pst[g, places, j * TOK : (j + 1) * TOK] = p.astype(BF16)
            mst[part, g, j : j + 1, :] = m
            lst[part, g, j : j + 1, :] = jnp.sum(p, axis=0, keepdims=True)

    q_in.wait()
    v_in.wait()

    def own(g, carry):
        scores(0, g)
        return carry

    lax.fori_loop(0, GROUPS, own, 0)
    pl.semaphore_wait(heard.at[0], len(near))
    tell(1, [at_z(2), at_z(-2), at_plane(NY // 2 * NC)])

    row16 = lax.rem(iota((2 * DOCS, TOK), 0), DOCS)

    def weigh(g):
        top = jnp.maximum(mst[0, g], mst[1, g])
        fs = [jnp.exp2(mst[part, g] - top) for part in range(2)]
        inv = 1.0 / (lst[0, g] * fs[0] + lst[1, g] * fs[1])
        lhs = []
        for f in fs:
            f = f * inv
            hi = f.astype(BF16).astype(F32)
            both = jnp.concatenate([hi, f - hi], axis=0)
            lhs.append(jnp.concatenate([jnp.where(row16 == j, both, 0.0).astype(BF16) for j in range(PER)], axis=1))
        acc = lax.dot_general(jnp.concatenate(lhs, axis=0), pst[g], NT, preferred_element_type=F32)
        for e in range(NX):
            at = 0 if e == 0 else 2 * DOCS
            half = acc[at : at + 2 * DOCS, e * TOK : (e + 1) * TOK]
            wo[g, :, pl.ds(pl.multiple_of(x_from(e) * TOK, TOK), TOK)] = half[:DOCS] + half[DOCS:]

    def key_copy(d, i):
        g = lax.rem(x + d + 1 + i, GROUPS)
        return copy(kb.at[g, 0], kb.at[g, d], k_s.at[d, i], k_r.at[d, i], at_x(d))

    def step(i, carry):
        group = lax.rem(x + 1 + i, GROUPS)

        for d in (1, 3, 2):
            key_copy(d, i).wait_recv()
        scores(1, group)
        weigh(group)

        @pl.when(i < GROUPS - 1)
        def _():
            copy(wo.at[group], wi.at[x], w_s.at[i + 1], w_r.at[i + 1], at_x(i + 1)).start()

        @pl.when(i == 0)
        def _():
            pl.semaphore_wait(heard.at[1], 3)
            tell(2, [at_z(4), at_z(-4)])

        return carry

    lax.fori_loop(0, GROUPS, step, 0)
    pl.semaphore_wait(heard.at[2], 2)
    for d in range(1, NX):
        group = lax.rem(x + d, GROUPS)
        w_copies[d] = copy(wo.at[group], wi.at[x], w_s.at[d], w_r.at[d], at_x(d))
    for k in range(1, PLANE):
        p_copies[k] = copy(prow.at[mine], prow.at[mine], p_s.at[k], p_r.at[k], at_plane(k))
        p_copies[k].start()
    onehot = (segment(iota((DOCS, WIN), 1)) == iota((DOCS, WIN), 0)).astype(F32)
    for d in (1, 3, 2):
        v_copies[d].wait_recv()
    weights = wo[x]
    for d in (1, 3, 2):
        w_copies[d].wait_recv()
        weights = weights + wi[x_from(d)]
    lhs = jnp.concatenate([weights[j : j + 1] * onehot for j in range(PER)], axis=0)
    hi, lo = split2(lhs)
    sums = jnp.dot(jnp.concatenate([hi, lo], axis=0), vb[...].reshape(WIN, D), preferred_element_type=F32)
    sums = sums[: PER * DOCS] + sums[PER * DOCS :]
    per_length = 1.0 / length
    for j in range(PER):
        pooled[:, j * D : (j + 1) * D] = sums[j * DOCS : (j + 1) * DOCS] * per_length
    short = pooled[...].astype(BF16)
    ucol[z] = short
    urow[mine] = short

    c_copies = {}
    u_copies = {}

    def send_col(origin, step, offset):
        c_copies[offset] = copy(ucol.at[origin], ucol.at[origin], c_s.at[offset % NZ], c_r.at[offset % NZ], at_z(step))
        c_copies[offset].start()

    for o in (5, -5, 7, -7, 8, 1, -1):
        send_col(z, o, o)
    for k in range(1, PLANE):
        u_copies[k] = copy(urow.at[mine], urow.at[mine], u_s.at[k], u_r.at[k], at_plane(k))
        u_copies[k].start()
    for o in FAR:
        c_copies[o].wait_recv()
        for step in FORWARD[o]:
            send_col(z_from(o), step, o + step)
    for k in range(1, PLANE):
        u_copies[k].wait_recv()

    def squares(a):
        wide = a.astype(F32)
        return jnp.sum(wide * wide, axis=1, keepdims=True)

    def to_row(column):
        n = column.shape[0]
        return jnp.sum(jnp.where(iota((n, D), 0) == iota((n, D), 1), column, 0.0), axis=0, keepdims=True)

    rows = urow[...].reshape(ROWS, FEAT)
    dsend[ROWS:, :] = jnp.broadcast_to(to_row(squares(rows)), (DOCS, D))
    for o in c_copies:
        if o not in FAR:
            c_copies[o].wait_recv()
    cols = ucol[...].reshape(COLS, FEAT)
    dsend[:ROWS, :] = lax.dot_general(rows, cols, NT, preferred_element_type=F32)
    dsend[ROWS : ROWS + 1, :] = to_row(squares(cols))
    d_copies = {d: copy(dsend, drecv.at[x], d_s.at[d], d_r.at[d], at_x(d)) for d in (2, 1, 3)}
    for d in d_copies:
        d_copies[d].start()
    for d in (1, 3, 2):
        d_copies[d].wait_recv()
    full = dsend[...]
    for d in range(1, NX):
        full = full + drecv[x_from(d)]

    r_id, c_id = iota((ROWS, COLS), 0), iota((ROWS, COLS), 1)
    eye = r_id == c_id

    def to_column(row):
        return jnp.sum(jnp.where(eye, row, 0.0), axis=1, keepdims=True)

    inv_rows = 1.0 / jnp.sqrt(to_column(full[ROWS + 1 : ROWS + 2]) + 1e-6)
    inv_cols = INV_TEMP / jnp.sqrt(full[ROWS : ROWS + 1] + 1e-6)
    logits = full[:ROWS] * (inv_rows * inv_cols)
    r_plane, r_doc = r_id // DOCS, lax.rem(r_id, DOCS)
    c_z, c_doc = c_id // DOCS, lax.rem(c_id, DOCS)
    same = (r_plane == mine) & (c_z == z) & (r_doc == c_doc)
    weight = jnp.where(same, 0.0, jnp.exp(logits))
    col_sum = jnp.sum(weight, axis=0, keepdims=True)
    ssend[...] = jnp.broadcast_to(col_sum, (DOCS, D))
    t_copies = {}
    a_copies = {}
    for o in (8, 7, -7, 6, -6, 5, -5, 4, -4, 3, -3, 2, -2, 1, -1):
        t_copies[o] = copy(ssend.at[pl.ds(0, 1)], scol.at[z, pl.ds(0, 1)], t_s.at[o % NZ], t_r.at[o % NZ], at_z(o))
        t_copies[o].start()
    row_sum = to_row(jnp.sum(weight, axis=1, keepdims=True))
    rsend[...] = jnp.broadcast_to(row_sum, (DOCS, D))
    for k in range(1, PLANE):
        a_copies[k] = copy(rsend.at[pl.ds(0, 1)], srow.at[mine, pl.ds(0, 1)], a_s.at[k], a_r.at[k], at_plane(k))
        a_copies[k].start()

    norms[...] = jnp.broadcast_to(inv_rows, (ROWS, D))
    own_inverse = norms[pl.ds(pl.multiple_of(mine * DOCS, DOCS), DOCS), :]
    for j in range(PER):
        at = slice(j * D, (j + 1) * D)
        out[:, at] = pooled[:, at] * own_inverse
    emb_out = pltpu.make_async_copy(out.at[:, pl.ds(0, FEAT)], out_hbm.at[:, pl.ds(0, FEAT)], osem.at[0])
    emb_out.start()
    for k in p_copies:
        p_copies[k].wait_recv()
    partners = prow[...].reshape(ROWS, D)
    column_doc = ((y * NZ + c_z) * NC + c) * DOCS + c_doc
    pairs = jnp.where(partners == column_doc.astype(F32), 2.0, 0.0)
    for k in range(1, PLANE):
        a_copies[k].wait_recv()
        row_sum = row_sum + srow[slot_from(k), 0:1, :]
    scale = inv_rows * inv_cols
    ready = (weight * (1.0 / to_column(row_sum)) - pairs) * scale
    scaled_weight = weight * scale
    undone = full[:ROWS] * inv_rows
    for o in reversed(list(t_copies)):
        t_copies[o].wait_recv()
        col_sum = col_sum + scol[z_from(o), 0:1, :]
    scaled = scaled_weight * (1.0 / col_sum) + ready
    along = jnp.sum(scaled * undone, axis=1, keepdims=True)
    hi, lo = split2(scaled)
    parts = jnp.dot(jnp.concatenate([hi, lo], axis=0), cols, preferred_element_type=F32)
    gsend[:, :, :FEAT] = (parts[:ROWS] + parts[ROWS:]).reshape(PLANE, DOCS, FEAT)
    gsend[:, :, FEAT:] = jnp.broadcast_to(along, (ROWS, D)).reshape(PLANE, DOCS, D)
    g_copies = {}
    for k in (5, 4, 7, 3, 6, 2, 1):
        g_copies[k] = copy(gsend.at[slot_to(k)], grecv.at[mine], g_s.at[k], g_r.at[k], at_plane(k))
        g_copies[k].start()
    gradient = gsend[mine].astype(F32)
    for k in range(1, PLANE):
        g_copies[k].wait_recv()
        gradient = gradient + grecv[slot_from(k)].astype(F32)
    out[:, FEAT:] = gradient
    grad_out = pltpu.make_async_copy(out.at[:, pl.ds(FEAT, FEAT + D)], out_hbm.at[:, pl.ds(FEAT, FEAT + D)], osem.at[1])
    grad_out.start()

    for copies in (
        k_copies, v_copies, p_copies, w_copies, c_copies, u_copies, d_copies, t_copies, a_copies, g_copies
    ):
        for key in copies:
            copies[key].wait_send()
    emb_out.wait()
    grad_out.wait()


def per_device(queries, keys, values, document_lengths, pair_ids):
    dma = pltpu.SemaphoreType.DMA
    hbm = pl.BlockSpec(memory_space=pl.ANY)
    both = pl.pallas_call(
        kernel,
        out_shape=jax.ShapeDtypeStruct((DOCS, 2 * FEAT + D), F32),
        in_specs=[hbm] * 5,
        out_specs=hbm,
        scratch_shapes=[
            pltpu.SMEM((1, DOCS), jnp.int32),
            pltpu.SMEM((DOCS,), jnp.int32),
            pltpu.VMEM((TOK, HEADS * D), BF16),
            pltpu.VMEM((GROUPS, NX, TOK, D), BF16),
            pltpu.VMEM((NX, TOK, D), BF16),
            pltpu.VMEM((WIN, TOK), F32),
            pltpu.VMEM((GROUPS, WIN, PER * TOK), BF16),
            pltpu.VMEM((2, GROUPS, DOCS, TOK), F32),
            pltpu.VMEM((2, GROUPS, DOCS, TOK), F32),
            pltpu.VMEM((GROUPS, DOCS, WIN), F32),
            pltpu.VMEM((NX, DOCS, WIN), F32),
            pltpu.VMEM((DOCS, FEAT), F32),
            pltpu.VMEM((NZ, DOCS, FEAT), BF16),
            pltpu.VMEM((PLANE, DOCS, FEAT), BF16),
            pltpu.VMEM((PLANE, DOCS, D), F32),
            pltpu.VMEM((ROWS + DOCS, COLS), F32),
            pltpu.VMEM((NX, ROWS + DOCS, COLS), F32),
            pltpu.VMEM((DOCS, D), F32),
            pltpu.VMEM((NZ, DOCS, D), F32),
            pltpu.VMEM((DOCS, D), F32),
            pltpu.VMEM((PLANE, DOCS, D), F32),
            pltpu.VMEM((PLANE, DOCS, FEAT + D), F32),
            pltpu.VMEM((PLANE, DOCS, FEAT + D), F32),
            pltpu.VMEM((ROWS, D), F32),
            pltpu.VMEM((DOCS, 2 * FEAT + D), F32),
            pltpu.SemaphoreType.REGULAR((3,)),
            dma((2,)),
            dma((4 + GROUPS,)),
            dma((NX, GROUPS)), dma((NX, GROUPS)),
            dma((NX,)), dma((NX,)),
            dma((NX,)), dma((NX,)),
            dma((PLANE,)), dma((PLANE,)),
            dma((PLANE,)), dma((PLANE,)),
            dma((NZ,)), dma((NZ,)),
            dma((NX,)), dma((NX,)),
            dma((NZ,)), dma((NZ,)),
            dma((PLANE,)), dma((PLANE,)),
            dma((PLANE,)), dma((PLANE,)),
        ],
        compiler_params=pltpu.CompilerParams(
            collective_id=0, has_side_effects=True, vmem_limit_bytes=60 << 20
        ),
    )(document_lengths, pair_ids, queries, keys, values)
    embeddings = both[:, :FEAT].astype(BF16)
    grads = both[:, FEAT : 2 * FEAT] - embeddings.astype(F32) * both[:, 2 * FEAT : 2 * FEAT + 1]
    return embeddings, grads


def solution(mesh):
    return jax.shard_map(
        per_device,
        mesh=mesh,
        in_specs=(
            P(("dp", "sp"), None),
            P(("dp", "sp"), None),
            P(("dp", "sp"), None),
            P("dp", None),
            P("dp"),
        ),
        out_specs=(P("dp", "sp"), P("dp", "sp")),
        check_vma=False,
    )
```

```python
import functools
import math

import jax
import jax.numpy as jnp
from jax import lax
from jax.experimental import pallas as pl
from jax.experimental.pallas import tpu as pltpu
from jax.sharding import PartitionSpec as P

MESH = pl.DeviceIdType.MESH
F32 = jnp.float32
BF16 = jnp.bfloat16
NT = (((1,), (1,)), ((), ()))

GROUPS = 4
PER = 7
HEADS = GROUPS * PER
D = 128
DOCS = 8
TOK = 128
WIN = 512
FEAT = PER * D
NX, NY, NZ, NC = 4, 4, 16, 2
PLANE = NY * NC
ROWS = PLANE * DOCS
COLS = NZ * DOCS
INV_TEMP = 50.0
SCALE2 = D ** (-0.5) * math.log2(math.e)

NEAR = ()
FAR = (1, -1, 5, -5)
FORWARD = {1: (1,), -1: (-1,), 5: (1, -2, -1), -5: (-1, 2, 1)}


def split2(a):
    hi = a.astype(BF16)
    return hi, (a - hi.astype(F32)).astype(BF16)


def kernel(
    lens_hbm, pair_hbm, q_hbm, k_hbm, v_hbm, out_hbm,
    lens, pair, qv, kb, vb, bias, pst, mst, lst, wo, wi, pooled, ucol, urow, prow,
    dsend, drecv, ssend, scol, rsend, srow, gsend, grecv, norms, out,
    heard, osem, lsem, k_s, k_r, v_s, v_r, w_s, w_r, p_s, p_r, u_s, u_r, c_s, c_r, d_s, d_r, t_s, t_r, a_s, a_r, g_s, g_r,
):
    dp = lax.axis_index("dp")
    x = lax.axis_index("sp")
    c = lax.rem(dp, NC)
    z = lax.rem(dp // NC, NZ)
    y = dp // (NC * NZ)
    mine = y * NC + c

    def at_x(d):
        return (dp, lax.rem(x + d, NX))

    def at_z(o):
        return ((y * NZ + lax.rem(z + o + NZ, NZ)) * NC + c, x)

    def at_plane(k):
        there_y, there_c = lax.rem(y + k // NC, NY), lax.rem(c + k % NC, NC)
        return ((there_y * NZ + z) * NC + there_c, x)

    def slot_to(k):
        return lax.rem(y + k // NC, NY) * NC + lax.rem(c + k % NC, NC)

    def slot_from(k):
        return lax.rem(y - k // NC + NY, NY) * NC + lax.rem(c + k % NC, NC)

    def z_from(o):
        return lax.rem(z - o + NZ, NZ)

    def x_from(d):
        return lax.rem(x - d + NX, NX)

    def copy(src, dst, ss, rs, there):
        return pltpu.make_async_remote_copy(
            src_ref=src, dst_ref=dst, send_sem=ss, recv_sem=rs, device_id=there, device_id_type=MESH
        )

    near = [at_plane(1), at_plane(NC), at_plane((NY - 1) * NC), at_z(1), at_z(-1)]
    barrier = pltpu.get_barrier_semaphore()
    for d in (2, 1, 3):
        pl.semaphore_signal(barrier, inc=1, device_id=at_x(d), device_id_type=MESH)
    for there in near:
        pl.semaphore_signal(barrier, inc=1, device_id=there, device_id_type=MESH)

    def tell(level, others):
        for there in others:
            pl.semaphore_signal(heard.at[level], inc=1, device_id=there, device_id_type=MESH)

    lens_in = pltpu.make_async_copy(lens_hbm, lens, lsem.at[0])
    pair_in = pltpu.make_async_copy(pair_hbm, pair, lsem.at[1])
    q_in = pltpu.make_async_copy(q_hbm, qv, lsem.at[2])
    v_in = pltpu.make_async_copy(v_hbm.at[:, pl.ds(pl.multiple_of(x * D, D), D)], vb.at[x], lsem.at[3])
    k_in = [
        pltpu.make_async_copy(k_hbm.at[:, g * D : (g + 1) * D], kb.at[g, 0], lsem.at[4 + g]) for g in range(GROUPS)
    ]
    for one in k_in:
        one.start()
    lens_in.start()
    pair_in.start()
    q_in.start()
    v_in.start()
    for one in k_in:
        one.wait()
    pl.semaphore_wait(barrier, NX - 1 + len(near))

    k_copies = {}
    v_copies = {}
    p_copies = {}
    w_copies = {}
    for i in range(GROUPS):
        for d in (1, 3, 2):
            g = lax.rem(x + d + 1 + i, GROUPS)
            k_copies[d, i] = copy(kb.at[g, 0], kb.at[g, d], k_s.at[d, i], k_r.at[d, i], at_x(d))
            k_copies[d, i].start()
    for d in (1, 3, 2):
        there = lax.rem(x + d, NX)
        v_copies[d] = copy(
            v_hbm.at[:, pl.ds(pl.multiple_of(there * D, D), D)], vb.at[x], v_s.at[d], v_r.at[d], at_x(d)
        )
        v_copies[d].start()
    tell(0, near)
    lens_in.wait()
    pair_in.wait()

    ends = []
    total = 0
    for i in range(DOCS):
        total = total + lens[0, i]
        ends.append(total)

    def segment(places):
        out = jnp.zeros(places.shape, jnp.int32)
        for end in ends:
            out = out + (places >= end).astype(jnp.int32)
        return out

    def iota(shape, axis):
        return lax.broadcasted_iota(jnp.int32, shape, axis)

    q_segment = segment(x * TOK + iota((TOK, TOK), 1))
    row8 = iota((DOCS, D), 0)
    length = jnp.zeros((DOCS, D), F32)
    partner = jnp.zeros((DOCS, D), F32)
    for i in range(DOCS):
        length = jnp.where(row8 == i, lens[0, i].astype(F32), length)
        partner = jnp.where(row8 == i, pair[i].astype(F32), partner)
    prow[mine] = partner
    mst[...] = jnp.zeros_like(mst)
    lst[...] = jnp.ones_like(lst)

    for e in range(NX):
        k_segment = segment(x_from(e) * TOK + iota((TOK, TOK), 0))
        bias[e * TOK : (e + 1) * TOK] = jnp.where(k_segment == q_segment, 0.0, -1e30).astype(F32)

    def scores(part, g):
        places = slice(0, TOK) if part == 0 else slice(TOK, WIN)
        key = kb[g, 0] if part == 0 else kb[g, 1:].reshape(WIN - TOK, D)
        for j in range(PER):
            query = qv[:, pl.ds(pl.multiple_of((g * PER + j) * D, D), D)]
            s = lax.dot_general(key, query, NT, preferred_element_type=F32) * SCALE2 + bias[places]
            m = jnp.max(s, axis=0, keepdims=True)
            p = jnp.exp2(s - m)
            pst[g, places, j * TOK : (j + 1) * TOK] = p.astype(BF16)
            mst[part, g, j : j + 1, :] = m
            lst[part, g, j : j + 1, :] = jnp.sum(p, axis=0, keepdims=True)

    q_in.wait()
    v_in.wait()

    def own(g, carry):
        scores(0, g)
        return carry

    lax.fori_loop(0, GROUPS, own, 0)
    pl.semaphore_wait(heard.at[0], len(near))
    tell(1, [at_z(2), at_z(-2), at_plane(NY // 2 * NC)])

    row16 = lax.rem(iota((2 * DOCS, TOK), 0), DOCS)

    def weigh(g):
        top = jnp.maximum(mst[0, g], mst[1, g])
        fs = [jnp.exp2(mst[part, g] - top) for part in range(2)]
        inv = 1.0 / (lst[0, g] * fs[0] + lst[1, g] * fs[1])
        lhs = []
        for f in fs:
            f = f * inv
            hi = f.astype(BF16).astype(F32)
            both = jnp.concatenate([hi, f - hi], axis=0)
            lhs.append(jnp.concatenate([jnp.where(row16 == j, both, 0.0).astype(BF16) for j in range(PER)], axis=1))
        acc = lax.dot_general(jnp.concatenate(lhs, axis=0), pst[g], NT, preferred_element_type=F32)
        for e in range(NX):
            at = 0 if e == 0 else 2 * DOCS
            half = acc[at : at + 2 * DOCS, e * TOK : (e + 1) * TOK]
            wo[g, :, pl.ds(pl.multiple_of(x_from(e) * TOK, TOK), TOK)] = half[:DOCS] + half[DOCS:]

    def key_copy(d, i):
        g = lax.rem(x + d + 1 + i, GROUPS)
        return copy(kb.at[g, 0], kb.at[g, d], k_s.at[d, i], k_r.at[d, i], at_x(d))

    def step(i, carry):
        group = lax.rem(x + 1 + i, GROUPS)

        for d in (1, 3, 2):
            key_copy(d, i).wait_recv()
        scores(1, group)
        weigh(group)

        @pl.when(i < GROUPS - 1)
        def _():
            copy(wo.at[group], wi.at[x], w_s.at[i + 1], w_r.at[i + 1], at_x(i + 1)).start()

        @pl.when(i == 0)
        def _():
            pl.semaphore_wait(heard.at[1], 3)
            tell(2, [at_z(4), at_z(-4)])

        return carry

    lax.fori_loop(0, GROUPS, step, 0)
    pl.semaphore_wait(heard.at[2], 2)
    for d in range(1, NX):
        group = lax.rem(x + d, GROUPS)
        w_copies[d] = copy(wo.at[group], wi.at[x], w_s.at[d], w_r.at[d], at_x(d))
    for k in range(1, PLANE):
        p_copies[k] = copy(prow.at[mine], prow.at[mine], p_s.at[k], p_r.at[k], at_plane(k))
        p_copies[k].start()
    onehot = (segment(iota((DOCS, WIN), 1)) == iota((DOCS, WIN), 0)).astype(F32)
    for d in (1, 3, 2):
        v_copies[d].wait_recv()
    weights = wo[x]
    for d in (1, 3, 2):
        w_copies[d].wait_recv()
        weights = weights + wi[x_from(d)]
    lhs = jnp.concatenate([weights[j : j + 1] * onehot for j in range(PER)], axis=0)
    hi, lo = split2(lhs)
    sums = jnp.dot(jnp.concatenate([hi, lo], axis=0), vb[...].reshape(WIN, D), preferred_element_type=F32)
    sums = sums[: PER * DOCS] + sums[PER * DOCS :]
    per_length = 1.0 / length
    for j in range(PER):
        pooled[:, j * D : (j + 1) * D] = sums[j * DOCS : (j + 1) * DOCS] * per_length
    short = pooled[...].astype(BF16)
    ucol[z] = short
    urow[mine] = short

    c_copies = {}
    u_copies = {}

    def send_col(origin, step, offset):
        c_copies[offset] = copy(ucol.at[origin], ucol.at[origin], c_s.at[offset % NZ], c_r.at[offset % NZ], at_z(step))
        c_copies[offset].start()

    for o in (5, -5, 7, -7, 8, 1, -1):
        send_col(z, o, o)
    for k in range(1, PLANE):
        u_copies[k] = copy(urow.at[mine], urow.at[mine], u_s.at[k], u_r.at[k], at_plane(k))
        u_copies[k].start()
    for o in FAR:
        c_copies[o].wait_recv()
        for step in FORWARD[o]:
            send_col(z_from(o), step, o + step)
    for k in range(1, PLANE):
        u_copies[k].wait_recv()

    def squares(a):
        wide = a.astype(F32)
        return jnp.sum(wide * wide, axis=1, keepdims=True)

    def to_row(column):
        n = column.shape[0]
        return jnp.sum(jnp.where(iota((n, D), 0) == iota((n, D), 1), column, 0.0), axis=0, keepdims=True)

    rows = urow[...].reshape(ROWS, FEAT)
    dsend[ROWS:, :] = jnp.broadcast_to(to_row(squares(rows)), (DOCS, D))
    for o in c_copies:
        if o not in FAR:
            c_copies[o].wait_recv()
    cols = ucol[...].reshape(COLS, FEAT)
    dsend[:ROWS, :] = lax.dot_general(rows, cols, NT, preferred_element_type=F32)
    dsend[ROWS : ROWS + 1, :] = to_row(squares(cols))
    d_copies = {d: copy(dsend, drecv.at[x], d_s.at[d], d_r.at[d], at_x(d)) for d in (2, 1, 3)}
    for d in d_copies:
        d_copies[d].start()
    for d in (1, 3, 2):
        d_copies[d].wait_recv()
    full = dsend[...]
    for d in range(1, NX):
        full = full + drecv[x_from(d)]

    r_id, c_id = iota((ROWS, COLS), 0), iota((ROWS, COLS), 1)
    eye = r_id == c_id

    def to_column(row):
        return jnp.sum(jnp.where(eye, row, 0.0), axis=1, keepdims=True)

    inv_rows = 1.0 / jnp.sqrt(to_column(full[ROWS + 1 : ROWS + 2]) + 1e-6)
    inv_cols = INV_TEMP / jnp.sqrt(full[ROWS : ROWS + 1] + 1e-6)
    logits = full[:ROWS] * (inv_rows * inv_cols)
    r_plane, r_doc = r_id // DOCS, lax.rem(r_id, DOCS)
    c_z, c_doc = c_id // DOCS, lax.rem(c_id, DOCS)
    same = (r_plane == mine) & (c_z == z) & (r_doc == c_doc)
    weight = jnp.where(same, 0.0, jnp.exp(logits))
    col_sum = jnp.sum(weight, axis=0, keepdims=True)
    ssend[...] = jnp.broadcast_to(col_sum, (DOCS, D))
    t_copies = {}
    a_copies = {}
    for o in (8, 7, -7, 6, -6, 5, -5, 4, -4, 3, -3, 2, -2, 1, -1):
        t_copies[o] = copy(ssend.at[pl.ds(0, 1)], scol.at[z, pl.ds(0, 1)], t_s.at[o % NZ], t_r.at[o % NZ], at_z(o))
        t_copies[o].start()
    row_sum = to_row(jnp.sum(weight, axis=1, keepdims=True))
    rsend[...] = jnp.broadcast_to(row_sum, (DOCS, D))
    for k in range(1, PLANE):
        a_copies[k] = copy(rsend.at[pl.ds(0, 1)], srow.at[mine, pl.ds(0, 1)], a_s.at[k], a_r.at[k], at_plane(k))
        a_copies[k].start()

    norms[...] = jnp.broadcast_to(inv_rows, (ROWS, D))
    own_inverse = norms[pl.ds(pl.multiple_of(mine * DOCS, DOCS), DOCS), :]
    for j in range(PER):
        at = slice(j * D, (j + 1) * D)
        out[:, at] = pooled[:, at] * own_inverse
    emb_out = pltpu.make_async_copy(out.at[:, pl.ds(0, FEAT)], out_hbm.at[:, pl.ds(0, FEAT)], osem.at[0])
    emb_out.start()
    for k in p_copies:
        p_copies[k].wait_recv()
    partners = prow[...].reshape(ROWS, D)
    column_doc = ((y * NZ + c_z) * NC + c) * DOCS + c_doc
    pairs = jnp.where(partners == column_doc.astype(F32), 2.0, 0.0)
    for k in range(1, PLANE):
        a_copies[k].wait_recv()
        row_sum = row_sum + srow[slot_from(k), 0:1, :]
    scale = inv_rows * inv_cols
    ready = (weight * (1.0 / to_column(row_sum)) - pairs) * scale
    scaled_weight = weight * scale
    undone = full[:ROWS] * inv_rows
    for o in reversed(list(t_copies)):
        t_copies[o].wait_recv()
        col_sum = col_sum + scol[z_from(o), 0:1, :]
    scaled = scaled_weight * (1.0 / col_sum) + ready
    along = jnp.sum(scaled * undone, axis=1, keepdims=True)
    hi, lo = split2(scaled)
    parts = jnp.dot(jnp.concatenate([hi, lo], axis=0), cols, preferred_element_type=F32)
    gsend[:, :, :FEAT] = (parts[:ROWS] + parts[ROWS:]).astype(BF16).reshape(PLANE, DOCS, FEAT)
    high, low = split2(along)
    sides = jnp.where(c_id < D // 2, high.astype(F32), low.astype(F32))
    gsend[:, :, FEAT:] = sides.astype(BF16).reshape(PLANE, DOCS, D)
    g_copies = {}
    for k in (5, 4, 7, 3, 6, 2, 1):
        g_copies[k] = copy(gsend.at[slot_to(k)], grecv.at[mine], g_s.at[k], g_r.at[k], at_plane(k))
        g_copies[k].start()
    gradient = gsend[mine].astype(F32)
    for k in range(1, PLANE):
        g_copies[k].wait_recv()
        gradient = gradient + grecv[slot_from(k)].astype(F32)
    out[:, FEAT:] = gradient
    grad_out = pltpu.make_async_copy(out.at[:, pl.ds(FEAT, FEAT + D)], out_hbm.at[:, pl.ds(FEAT, FEAT + D)], osem.at[1])
    grad_out.start()

    for copies in (
        k_copies, v_copies, p_copies, w_copies, c_copies, u_copies, d_copies, t_copies, a_copies, g_copies
    ):
        for key in copies:
            copies[key].wait_send()
    emb_out.wait()
    grad_out.wait()


def per_device(queries, keys, values, document_lengths, pair_ids):
    dma = pltpu.SemaphoreType.DMA
    hbm = pl.BlockSpec(memory_space=pl.ANY)
    both = pl.pallas_call(
        kernel,
        out_shape=jax.ShapeDtypeStruct((DOCS, 2 * FEAT + D), F32),
        in_specs=[hbm] * 5,
        out_specs=hbm,
        scratch_shapes=[
            pltpu.SMEM((1, DOCS), jnp.int32),
            pltpu.SMEM((DOCS,), jnp.int32),
            pltpu.VMEM((TOK, HEADS * D), BF16),
            pltpu.VMEM((GROUPS, NX, TOK, D), BF16),
            pltpu.VMEM((NX, TOK, D), BF16),
            pltpu.VMEM((WIN, TOK), F32),
            pltpu.VMEM((GROUPS, WIN, PER * TOK), BF16),
            pltpu.VMEM((2, GROUPS, DOCS, TOK), F32),
            pltpu.VMEM((2, GROUPS, DOCS, TOK), F32),
            pltpu.VMEM((GROUPS, DOCS, WIN), F32),
            pltpu.VMEM((NX, DOCS, WIN), F32),
            pltpu.VMEM((DOCS, FEAT), F32),
            pltpu.VMEM((NZ, DOCS, FEAT), BF16),
            pltpu.VMEM((PLANE, DOCS, FEAT), BF16),
            pltpu.VMEM((PLANE, DOCS, D), F32),
            pltpu.VMEM((ROWS + DOCS, COLS), F32),
            pltpu.VMEM((NX, ROWS + DOCS, COLS), F32),
            pltpu.VMEM((DOCS, D), F32),
            pltpu.VMEM((NZ, DOCS, D), F32),
            pltpu.VMEM((DOCS, D), F32),
            pltpu.VMEM((PLANE, DOCS, D), F32),
            pltpu.VMEM((PLANE, DOCS, FEAT + D), BF16),
            pltpu.VMEM((PLANE, DOCS, FEAT + D), BF16),
            pltpu.VMEM((ROWS, D), F32),
            pltpu.VMEM((DOCS, 2 * FEAT + D), F32),
            pltpu.SemaphoreType.REGULAR((3,)),
            dma((2,)),
            dma((4 + GROUPS,)),
            dma((NX, GROUPS)), dma((NX, GROUPS)),
            dma((NX,)), dma((NX,)),
            dma((NX,)), dma((NX,)),
            dma((PLANE,)), dma((PLANE,)),
            dma((PLANE,)), dma((PLANE,)),
            dma((NZ,)), dma((NZ,)),
            dma((NX,)), dma((NX,)),
            dma((NZ,)), dma((NZ,)),
            dma((PLANE,)), dma((PLANE,)),
            dma((PLANE,)), dma((PLANE,)),
        ],
        compiler_params=pltpu.CompilerParams(
            collective_id=0, has_side_effects=True, vmem_limit_bytes=60 << 20
        ),
    )(document_lengths, pair_ids, queries, keys, values)
    embeddings = both[:, :FEAT].astype(BF16)
    side = both[:, 2 * FEAT :]
    grads = both[:, FEAT : 2 * FEAT] - embeddings.astype(F32) * (side[:, :1] + side[:, D // 2 : D // 2 + 1])
    return embeddings, grads


def solution(mesh):
    return jax.shard_map(
        per_device,
        mesh=mesh,
        in_specs=(
            P(("dp", "sp"), None),
            P(("dp", "sp"), None),
            P(("dp", "sp"), None),
            P("dp", None),
            P("dp"),
        ),
        out_specs=(P("dp", "sp"), P("dp", "sp")),
        check_vma=False,
    )
```

```python
import functools
import math

import jax
import jax.numpy as jnp
from jax import lax
from jax.experimental import pallas as pl
from jax.experimental.pallas import tpu as pltpu
from jax.sharding import PartitionSpec as P

MESH = pl.DeviceIdType.MESH
F32 = jnp.float32
BF16 = jnp.bfloat16
NT = (((1,), (1,)), ((), ()))

GROUPS = 4
PER = 7
HEADS = GROUPS * PER
D = 128
DOCS = 8
TOK = 128
WIN = 512
FEAT = PER * D
NX, NY, NZ, NC = 4, 4, 16, 2
PLANE = NY * NC
ROWS = PLANE * DOCS
COLS = NZ * DOCS
INV_TEMP = 50.0
SCALE2 = D ** (-0.5) * math.log2(math.e)

NEAR = ()
FAR = (1, -1, 5, -5)
FORWARD = {1: (1,), -1: (-1,), 5: (1, -2, -1), -5: (-1, 2, 1)}


def split2(a):
    hi = a.astype(BF16)
    return hi, (a - hi.astype(F32)).astype(BF16)


def kernel(
    lens_hbm, pair_hbm, q_hbm, k_hbm, v_hbm, out_hbm,
    lens, pair, qv, kb, vb, bias, pst, mst, lst, wo, wi, pooled, ucol, urow, prow,
    dsend, drecv, ssend, scol, rsend, srow, gsend, grecv, norms, out,
    heard, osem, lsem, k_s, k_r, v_s, v_r, w_s, w_r, p_s, p_r, u_s, u_r, c_s, c_r, d_s, d_r, t_s, t_r, a_s, a_r, g_s, g_r,
):
    dp = lax.axis_index("dp")
    x = lax.axis_index("sp")
    c = lax.rem(dp, NC)
    z = lax.rem(dp // NC, NZ)
    y = dp // (NC * NZ)
    mine = y * NC + c

    def at_x(d):
        return (dp, lax.rem(x + d, NX))

    def at_z(o):
        return ((y * NZ + lax.rem(z + o + NZ, NZ)) * NC + c, x)

    def at_plane(k):
        there_y, there_c = lax.rem(y + k // NC, NY), lax.rem(c + k % NC, NC)
        return ((there_y * NZ + z) * NC + there_c, x)

    def slot_to(k):
        return lax.rem(y + k // NC, NY) * NC + lax.rem(c + k % NC, NC)

    def slot_from(k):
        return lax.rem(y - k // NC + NY, NY) * NC + lax.rem(c + k % NC, NC)

    def z_from(o):
        return lax.rem(z - o + NZ, NZ)

    def x_from(d):
        return lax.rem(x - d + NX, NX)

    def copy(src, dst, ss, rs, there):
        return pltpu.make_async_remote_copy(
            src_ref=src, dst_ref=dst, send_sem=ss, recv_sem=rs, device_id=there, device_id_type=MESH
        )

    near = [at_plane(1), at_plane(NC), at_plane((NY - 1) * NC), at_z(1), at_z(-1)]
    barrier = pltpu.get_barrier_semaphore()
    for d in (2, 1, 3):
        pl.semaphore_signal(barrier, inc=1, device_id=at_x(d), device_id_type=MESH)
    for there in near:
        pl.semaphore_signal(barrier, inc=1, device_id=there, device_id_type=MESH)

    def tell(level, others):
        for there in others:
            pl.semaphore_signal(heard.at[level], inc=1, device_id=there, device_id_type=MESH)

    lens_in = pltpu.make_async_copy(lens_hbm, lens, lsem.at[0])
    pair_in = pltpu.make_async_copy(pair_hbm, pair, lsem.at[1])
    q_in = pltpu.make_async_copy(q_hbm, qv, lsem.at[2])
    v_in = pltpu.make_async_copy(v_hbm.at[:, pl.ds(pl.multiple_of(x * D, D), D)], vb.at[x], lsem.at[3])
    k_in = [
        pltpu.make_async_copy(k_hbm.at[:, g * D : (g + 1) * D], kb.at[g, 0], lsem.at[4 + g]) for g in range(GROUPS)
    ]
    for one in k_in:
        one.start()
    lens_in.start()
    pair_in.start()
    q_in.start()
    v_in.start()
    for one in k_in:
        one.wait()
    pl.semaphore_wait(barrier, NX - 1 + len(near))

    k_copies = {}
    v_copies = {}
    p_copies = {}
    w_copies = {}
    for i in range(GROUPS):
        for d in (1, 3, 2):
            g = lax.rem(x + d + 1 + i, GROUPS)
            k_copies[d, i] = copy(kb.at[g, 0], kb.at[g, d], k_s.at[d, i], k_r.at[d, i], at_x(d))
            k_copies[d, i].start()
    for d in (1, 3, 2):
        there = lax.rem(x + d, NX)
        v_copies[d] = copy(
            v_hbm.at[:, pl.ds(pl.multiple_of(there * D, D), D)], vb.at[x], v_s.at[d], v_r.at[d], at_x(d)
        )
        v_copies[d].start()
    tell(0, near)
    lens_in.wait()
    pair_in.wait()

    ends = []
    total = 0
    for i in range(DOCS):
        total = total + lens[0, i]
        ends.append(total)

    def segment(places):
        out = jnp.zeros(places.shape, jnp.int32)
        for end in ends:
            out = out + (places >= end).astype(jnp.int32)
        return out

    def iota(shape, axis):
        return lax.broadcasted_iota(jnp.int32, shape, axis)

    q_segment = segment(x * TOK + iota((TOK, TOK), 1))
    row8 = iota((DOCS, D), 0)
    length = jnp.zeros((DOCS, D), F32)
    partner = jnp.zeros((DOCS, D), F32)
    for i in range(DOCS):
        length = jnp.where(row8 == i, lens[0, i].astype(F32), length)
        partner = jnp.where(row8 == i, pair[i].astype(F32), partner)
    prow[mine] = partner
    mst[...] = jnp.zeros_like(mst)
    lst[...] = jnp.ones_like(lst)

    for e in range(NX):
        k_segment = segment(x_from(e) * TOK + iota((TOK, TOK), 0))
        bias[e * TOK : (e + 1) * TOK] = jnp.where(k_segment == q_segment, 0.0, -1e30).astype(F32)

    def scores(part, g):
        places = slice(0, TOK) if part == 0 else slice(TOK, WIN)
        key = kb[g, 0] if part == 0 else kb[g, 1:].reshape(WIN - TOK, D)
        for j in range(PER):
            query = qv[:, pl.ds(pl.multiple_of((g * PER + j) * D, D), D)]
            s = lax.dot_general(key, query, NT, preferred_element_type=F32) * SCALE2 + bias[places]
            m = jnp.max(s, axis=0, keepdims=True)
            p = jnp.exp2(s - m)
            pst[g, places, j * TOK : (j + 1) * TOK] = p.astype(BF16)
            mst[part, g, j : j + 1, :] = m
            lst[part, g, j : j + 1, :] = jnp.sum(p, axis=0, keepdims=True)

    q_in.wait()
    v_in.wait()

    def own(g, carry):
        scores(0, g)
        return carry

    lax.fori_loop(0, GROUPS, own, 0)
    pl.semaphore_wait(heard.at[0], len(near))
    tell(1, [at_z(2), at_z(-2), at_plane(NY // 2 * NC)])

    row16 = lax.rem(iota((2 * DOCS, TOK), 0), DOCS)

    def weigh(g):
        top = jnp.maximum(mst[0, g], mst[1, g])
        fs = [jnp.exp2(mst[part, g] - top) for part in range(2)]
        inv = 1.0 / (lst[0, g] * fs[0] + lst[1, g] * fs[1])
        lhs = []
        for f in fs:
            f = f * inv
            hi = f.astype(BF16).astype(F32)
            both = jnp.concatenate([hi, f - hi], axis=0)
            lhs.append(jnp.concatenate([jnp.where(row16 == j, both, 0.0).astype(BF16) for j in range(PER)], axis=1))
        acc = lax.dot_general(jnp.concatenate(lhs, axis=0), pst[g], NT, preferred_element_type=F32)
        for e in range(NX):
            at = 0 if e == 0 else 2 * DOCS
            half = acc[at : at + 2 * DOCS, e * TOK : (e + 1) * TOK]
            wo[g, :, pl.ds(pl.multiple_of(x_from(e) * TOK, TOK), TOK)] = half[:DOCS] + half[DOCS:]

    def key_copy(d, i):
        g = lax.rem(x + d + 1 + i, GROUPS)
        return copy(kb.at[g, 0], kb.at[g, d], k_s.at[d, i], k_r.at[d, i], at_x(d))

    def step(i, carry):
        group = lax.rem(x + 1 + i, GROUPS)

        for d in (1, 3, 2):
            key_copy(d, i).wait_recv()
        scores(1, group)
        weigh(group)

        @pl.when(i < GROUPS - 1)
        def _():
            copy(wo.at[group], wi.at[x], w_s.at[i + 1], w_r.at[i + 1], at_x(i + 1)).start()

        @pl.when(i == 0)
        def _():
            pl.semaphore_wait(heard.at[1], 3)
            tell(2, [at_z(4), at_z(-4)])

        return carry

    lax.fori_loop(0, GROUPS, step, 0)
    pl.semaphore_wait(heard.at[2], 2)
    for d in range(1, NX):
        group = lax.rem(x + d, GROUPS)
        w_copies[d] = copy(wo.at[group], wi.at[x], w_s.at[d], w_r.at[d], at_x(d))
    for k in range(1, PLANE):
        p_copies[k] = copy(prow.at[mine], prow.at[mine], p_s.at[k], p_r.at[k], at_plane(k))
        p_copies[k].start()
    onehot = (segment(iota((DOCS, WIN), 1)) == iota((DOCS, WIN), 0)).astype(F32)
    for d in (1, 3, 2):
        v_copies[d].wait_recv()
    weights = wo[x]
    for d in (1, 3, 2):
        w_copies[d].wait_recv()
        weights = weights + wi[x_from(d)]
    lhs = jnp.concatenate([weights[j : j + 1] * onehot for j in range(PER)], axis=0)
    hi, lo = split2(lhs)
    sums = jnp.dot(jnp.concatenate([hi, lo], axis=0), vb[...].reshape(WIN, D), preferred_element_type=F32)
    sums = sums[: PER * DOCS] + sums[PER * DOCS :]
    per_length = 1.0 / length
    for j in range(PER):
        pooled[:, j * D : (j + 1) * D] = sums[j * DOCS : (j + 1) * DOCS] * per_length
    short = pooled[...].astype(BF16)
    ucol[z] = short
    urow[mine] = short

    c_copies = {}
    u_copies = {}

    def send_col(origin, step, offset):
        c_copies[offset] = copy(ucol.at[origin], ucol.at[origin], c_s.at[offset % NZ], c_r.at[offset % NZ], at_z(step))
        c_copies[offset].start()

    for o in (5, -5, 7, -7, 8, 1, -1):
        send_col(z, o, o)
    for k in range(1, PLANE):
        u_copies[k] = copy(urow.at[mine], urow.at[mine], u_s.at[k], u_r.at[k], at_plane(k))
        u_copies[k].start()
    for o in FAR:
        c_copies[o].wait_recv()
        for step in FORWARD[o]:
            send_col(z_from(o), step, o + step)
    for k in range(1, PLANE):
        u_copies[k].wait_recv()

    def squares(a):
        wide = a.astype(F32)
        return jnp.sum(wide * wide, axis=1, keepdims=True)

    def to_row(column):
        n = column.shape[0]
        return jnp.sum(jnp.where(iota((n, D), 0) == iota((n, D), 1), column, 0.0), axis=0, keepdims=True)

    rows = urow[...].reshape(ROWS, FEAT)
    dsend[ROWS:, :] = jnp.broadcast_to(to_row(squares(rows)), (DOCS, D))
    for o in c_copies:
        if o not in FAR:
            c_copies[o].wait_recv()
    cols = ucol[...].reshape(COLS, FEAT)
    dsend[:ROWS, :] = lax.dot_general(rows, cols, NT, preferred_element_type=F32)
    dsend[ROWS : ROWS + 1, :] = to_row(squares(cols))
    d_copies = {d: copy(dsend, drecv.at[x], d_s.at[d], d_r.at[d], at_x(d)) for d in (2, 1, 3)}
    for d in d_copies:
        d_copies[d].start()
    for d in (1, 3, 2):
        d_copies[d].wait_recv()
    full = dsend[...]
    for d in range(1, NX):
        full = full + drecv[x_from(d)]

    r_id, c_id = iota((ROWS, COLS), 0), iota((ROWS, COLS), 1)
    eye = r_id == c_id

    def to_column(row):
        return jnp.sum(jnp.where(eye, row, 0.0), axis=1, keepdims=True)

    inv_rows = 1.0 / jnp.sqrt(to_column(full[ROWS + 1 : ROWS + 2]) + 1e-6)
    inv_cols = INV_TEMP / jnp.sqrt(full[ROWS : ROWS + 1] + 1e-6)
    logits = full[:ROWS] * (inv_rows * inv_cols)
    r_plane, r_doc = r_id // DOCS, lax.rem(r_id, DOCS)
    c_z, c_doc = c_id // DOCS, lax.rem(c_id, DOCS)
    same = (r_plane == mine) & (c_z == z) & (r_doc == c_doc)
    weight = jnp.where(same, 0.0, jnp.exp(logits))
    col_sum = jnp.sum(weight, axis=0, keepdims=True)
    ssend[...] = jnp.broadcast_to(col_sum, (DOCS, D))
    t_copies = {}
    a_copies = {}
    for o in (8, 7, -7, 6, -6, 5, -5, 4, -4, 3, -3, 2, -2, 1, -1):
        t_copies[o] = copy(ssend.at[pl.ds(0, 1)], scol.at[z, pl.ds(0, 1)], t_s.at[o % NZ], t_r.at[o % NZ], at_z(o))
        t_copies[o].start()
    row_sum = to_row(jnp.sum(weight, axis=1, keepdims=True))
    rsend[...] = jnp.broadcast_to(row_sum, (DOCS, D))
    for k in range(1, PLANE):
        a_copies[k] = copy(rsend.at[pl.ds(0, 1)], srow.at[mine, pl.ds(0, 1)], a_s.at[k], a_r.at[k], at_plane(k))
        a_copies[k].start()

    norms[...] = jnp.broadcast_to(inv_rows, (ROWS, D))
    own_inverse = norms[pl.ds(pl.multiple_of(mine * DOCS, DOCS), DOCS), :]
    for j in range(PER):
        at = slice(j * D, (j + 1) * D)
        out[:, at] = pooled[:, at] * own_inverse
    emb_out = pltpu.make_async_copy(out.at[:, pl.ds(0, FEAT)], out_hbm.at[:, pl.ds(0, FEAT)], osem.at[0])
    emb_out.start()
    for k in p_copies:
        p_copies[k].wait_recv()
    partners = prow[...].reshape(ROWS, D)
    column_doc = ((y * NZ + c_z) * NC + c) * DOCS + c_doc
    pairs = jnp.where(partners == column_doc.astype(F32), 2.0, 0.0)
    for k in range(1, PLANE):
        a_copies[k].wait_recv()
        row_sum = row_sum + srow[slot_from(k), 0:1, :]
    scale = inv_rows * inv_cols
    ready = (weight * (1.0 / to_column(row_sum)) - pairs) * scale
    scaled_weight = weight * scale
    undone = full[:ROWS] * inv_rows
    for o in reversed(list(t_copies)):
        t_copies[o].wait_recv()
        col_sum = col_sum + scol[z_from(o), 0:1, :]
    scaled = scaled_weight * (1.0 / col_sum) + ready
    along = jnp.sum(scaled * undone, axis=1, keepdims=True)
    hi, lo = split2(scaled)
    parts = jnp.dot(jnp.concatenate([hi, lo], axis=0), cols, preferred_element_type=F32)
    gsend[:, :, :FEAT] = (parts[:ROWS] + parts[ROWS:]).astype(BF16).reshape(PLANE, DOCS, FEAT)
    high, low = split2(along)
    sides = jnp.where(c_id < D // 2, high.astype(F32), low.astype(F32))
    gsend[:, :, FEAT:] = sides.astype(BF16).reshape(PLANE, DOCS, D)
    g_copies = {}
    for k in (5, 4, 7, 3, 6, 2, 1):
        g_copies[k] = copy(gsend.at[slot_to(k)], grecv.at[mine], g_s.at[k], g_r.at[k], at_plane(k))
        g_copies[k].start()
    gradient = gsend[mine].astype(F32)
    for k in range(1, PLANE):
        g_copies[k].wait_recv()
        gradient = gradient + grecv[slot_from(k)].astype(F32)
    out[:, FEAT : 2 * FEAT] = gradient[:, :FEAT]
    tail = gradient[:, FEAT:]
    out[:, 2 * FEAT :] = jnp.broadcast_to(tail[:, :1] + tail[:, D // 2 : D // 2 + 1], (DOCS, D))
    grad_out = pltpu.make_async_copy(out.at[:, pl.ds(FEAT, FEAT + D)], out_hbm.at[:, pl.ds(FEAT, FEAT + D)], osem.at[1])
    grad_out.start()

    for copies in (
        k_copies, v_copies, p_copies, w_copies, c_copies, u_copies, d_copies, t_copies, a_copies, g_copies
    ):
        for key in copies:
            copies[key].wait_send()
    emb_out.wait()
    grad_out.wait()


def per_device(queries, keys, values, document_lengths, pair_ids):
    dma = pltpu.SemaphoreType.DMA
    hbm = pl.BlockSpec(memory_space=pl.ANY)
    both = pl.pallas_call(
        kernel,
        out_shape=jax.ShapeDtypeStruct((DOCS, 2 * FEAT + D), F32),
        in_specs=[hbm] * 5,
        out_specs=hbm,
        scratch_shapes=[
            pltpu.SMEM((1, DOCS), jnp.int32),
            pltpu.SMEM((DOCS,), jnp.int32),
            pltpu.VMEM((TOK, HEADS * D), BF16),
            pltpu.VMEM((GROUPS, NX, TOK, D), BF16),
            pltpu.VMEM((NX, TOK, D), BF16),
            pltpu.VMEM((WIN, TOK), F32),
            pltpu.VMEM((GROUPS, WIN, PER * TOK), BF16),
            pltpu.VMEM((2, GROUPS, DOCS, TOK), F32),
            pltpu.VMEM((2, GROUPS, DOCS, TOK), F32),
            pltpu.VMEM((GROUPS, DOCS, WIN), F32),
            pltpu.VMEM((NX, DOCS, WIN), F32),
            pltpu.VMEM((DOCS, FEAT), F32),
            pltpu.VMEM((NZ, DOCS, FEAT), BF16),
            pltpu.VMEM((PLANE, DOCS, FEAT), BF16),
            pltpu.VMEM((PLANE, DOCS, D), F32),
            pltpu.VMEM((ROWS + DOCS, COLS), F32),
            pltpu.VMEM((NX, ROWS + DOCS, COLS), F32),
            pltpu.VMEM((DOCS, D), F32),
            pltpu.VMEM((NZ, DOCS, D), F32),
            pltpu.VMEM((DOCS, D), F32),
            pltpu.VMEM((PLANE, DOCS, D), F32),
            pltpu.VMEM((PLANE, DOCS, FEAT + D), BF16),
            pltpu.VMEM((PLANE, DOCS, FEAT + D), BF16),
            pltpu.VMEM((ROWS, D), F32),
            pltpu.VMEM((DOCS, 2 * FEAT + D), F32),
            pltpu.SemaphoreType.REGULAR((3,)),
            dma((2,)),
            dma((4 + GROUPS,)),
            dma((NX, GROUPS)), dma((NX, GROUPS)),
            dma((NX,)), dma((NX,)),
            dma((NX,)), dma((NX,)),
            dma((PLANE,)), dma((PLANE,)),
            dma((PLANE,)), dma((PLANE,)),
            dma((NZ,)), dma((NZ,)),
            dma((NX,)), dma((NX,)),
            dma((NZ,)), dma((NZ,)),
            dma((PLANE,)), dma((PLANE,)),
            dma((PLANE,)), dma((PLANE,)),
        ],
        compiler_params=pltpu.CompilerParams(
            collective_id=0, has_side_effects=True, vmem_limit_bytes=60 << 20
        ),
    )(document_lengths, pair_ids, queries, keys, values)
    embeddings = both[:, :FEAT].astype(BF16)
    grads = both[:, FEAT : 2 * FEAT] - embeddings.astype(F32) * both[:, 2 * FEAT : 2 * FEAT + 1]
    return embeddings, grads


def solution(mesh):
    return jax.shard_map(
        per_device,
        mesh=mesh,
        in_specs=(
            P(("dp", "sp"), None),
            P(("dp", "sp"), None),
            P(("dp", "sp"), None),
            P("dp", None),
            P("dp"),
        ),
        out_specs=(P("dp", "sp"), P("dp", "sp")),
        check_vma=False,
    )
```
